512 devices in a mesh: dp: 8 (over y_hi, x), expert: 64 (over z, y_lo, core).
Axes of the slice: x: 4, y: 4 (y_hi: 2, y_lo: 2; y = y_hi * 2 + y_lo), z: 16, core: 2. Of those that a mesh axis runs over, the one named last changes fastest.
Arguments:
- tokens: bfloat16 [8192, 4096], P('expert', 'dp'), may hold values from -6 to 6
- expert_ids: int32 [8192, 8], P('expert'), may hold values from 0 to 63, all different within a row; in each aligned block of 128 rows (0 to 127, 128 to 255, ...) at most 19 rows name the same one
- route_weight: float32 [8192, 8], P('expert'), may hold values from 0.1 to 1
- placement: int32 [64], replicated, may hold values from 0 to 63, each once
- swap_flag: int32 [32], replicated, may hold values 0 or 1
- gate_up: bfloat16 [64, 2, 768, 4096], P('expert', None, 'dp'), may hold values from -0.09375 to 0.09375
- down_weight: bfloat16 [64, 768, 4096], P('expert', None, 'dp'), may hold values from -0.21875 to 0.21875
Outputs:
- moe_out: bfloat16 [8192, 4096], P('expert', 'dp')
- column_load: float32 [64], replicated
- slot_gate_up: bfloat16 [64, 2, 768, 4096], P('expert', None, 'dp')
- slot_down: bfloat16 [64, 768, 4096], P('expert', None, 'dp')
The draws below stay inside these ranges and needn't reach their ends.
Inputs may be any that keep to these rules, and one draw needn't show every extreme that they name: `expert_ids`: within the rows of one device (aligned blocks of 128 tokens) no expert is chosen more than 19 times, and some expert is chosen exactly 19 times; a token's 8 experts differ. A permutation: expert e's weights are in slot placement[e]. swap_flag[p] = 1 means slots p and p + 32 exchange owners.
All inputs are finite; a program needn't handle non-finite values.
Results may differ from the reference program's by a relative error of at most 0.0057.
Values may be sent and summed in bfloat16 or wider, within the bound.
A program may use at most 128 MiB of HBM per device.

```python
import math
import jax
import jax.numpy as jnp
import numpy as np
from jax import lax

D = 4096
FFN = 768
TOPK = 8
TOK_DEV = 128
EXPERTS = 64
PAIRS = 32
CAP = 19
TOKENS = 8192
N_EXPERT = 64


def with_ends(values, own_key, low, high):
    longest = values.shape.index(max(values.shape))
    spots = []
    for shift in (0, 1):
        where = [jax.random.randint(jax.random.fold_in(own_key, axis), (), 0, length) for axis, length in enumerate(values.shape)]
        where[longest] = (where[longest] + shift) % values.shape[longest]
        spots.append(tuple(where))
    return values.at[spots[0]].set(low).at[spots[1]].set(high)


def levels(rng, dims, cuts, low, top_value):
    level, own = 1.0, jax.random.fold_in(rng, 6)
    for position, blocks in cuts:
        draws = jnp.exp(jax.random.uniform(jax.random.fold_in(own, position), (blocks,), jnp.float32, low / len(cuts), top_value / len(cuts)))
        level = level * jnp.repeat(draws, dims[position] // blocks).reshape([-1 if axis == position else 1 for axis in range(len(dims))])
    return level


def routed_block(stream_key, own, number, rows, amount, top, most, lean):
    order = jax.random.permutation(stream_key, amount)
    packed, usual = portions_of(amount, rows * top, most, lean, True), portions_of(amount, rows * top, most, lean, False)
    places = jnp.arange(amount)

    def named(sizes, offset_by):
        used = int((sizes > 0).sum())
        fixed = max(1, used // 4)
        shifted = fixed + (places - fixed + offset_by * (used - fixed)) % max(1, amount - fixed)
        return jnp.zeros((amount,), jnp.int32).at[order[jnp.where(places < fixed, places, shifted)]].set(jnp.asarray(sizes, jnp.int32))

    sizes = jnp.where(number % 4 == 0, named(packed, number // 4), named(usual, number - number // 4 - 1))
    mixed = jax.random.permutation(jax.random.fold_in(own, 3), amount)
    giver, receiver = mixed[0:amount // 2 * 2:2], mixed[1:amount // 2 * 2:2]
    slack = jnp.minimum(sizes[giver] - 1, most - sizes[receiver]) // 2
    slack = jnp.where((giver == order[0]) | (receiver == order[0]) | (sizes[receiver] == 0), 0, jnp.maximum(slack, 0))
    shifted = jax.random.randint(jax.random.fold_in(own, 4), (amount // 2,), 0, 1 << 20) % (slack + 1)
    sizes = sizes.at[giver].add(-shifted).at[receiver].add(shifted)
    members = jnp.searchsorted(jnp.cumsum(sizes), jnp.arange(rows * top), side="right").astype(jnp.int32)
    listing = members.reshape(top, rows).T
    listing = listing[jax.random.permutation(jax.random.fold_in(own, 1), rows)]
    offset_by = jax.random.randint(jax.random.fold_in(own, 2), (rows, 1), 0, top)
    return jnp.take_along_axis(listing, (jnp.arange(top)[None, :] + offset_by) % top, axis=1)


def portions_of(amount, total, most, skew, full):
    weights = [(1 << 20) // math.isqrt(grade ** skew) + 1 for grade in range(1, amount + 1)]
    largest = most if full else min(most, max(-(-total // amount), total * weights[0] // sum(weights)))
    least = 1 if total - largest >= amount - 1 else 0
    given, spare = [largest] + [least] * (amount - 1), total - largest - least * (amount - 1)
    while spare > 0:
        candidates = [i for i in range(1, amount) if given[i] < largest] or [i for i in range(1, amount) if given[i] < most]
        mass, budget = sum([weights[i] for i in candidates]), spare
        for i in candidates:
            addition = min(most - given[i], max(1, budget * weights[i] // mass), spare)
            given[i] = given[i] + addition
            spare = spare - addition
    return np.array(given)


def noise(own_key, extent, spread, most, pieces=(), kind=jnp.bfloat16):
    array = spread * jax.random.normal(own_key, extent, jnp.float32)
    if pieces:
        array = array * levels(own_key, extent, pieces, -0.22, 0.18)
    return jnp.clip(array, -most, most).astype(kind)


def setup_inputs(seed: int = 0) -> dict:
    arg_keys = jax.random.split(jax.random.key(seed), 8)
    tokens = noise(arg_keys[0], (TOKENS, D), 1.0, 6.0, ((0, 64), (1, 8)))
    expert_ids_keys = jax.random.split(jax.random.fold_in(arg_keys[1], 1), TOKENS // TOK_DEV)
    expert_ids_turns = jax.random.permutation(jax.random.fold_in(arg_keys[1], 3), TOKENS // TOK_DEV)
    expert_ids = jax.vmap(lambda own, number: routed_block(jax.random.fold_in(arg_keys[1], 2), own, number, TOK_DEV, EXPERTS, TOPK, CAP, 1))(expert_ids_keys, expert_ids_turns).reshape((TOKENS, TOPK))
    route_weight = jnp.clip(jnp.exp(math.log(1.0) - 2.3025851 * jax.random.uniform(arg_keys[2], (TOKENS, TOPK), jnp.float32) ** levels(arg_keys[2], (TOKENS, TOPK), ((0, 64),), -0.2, 0.2)), 0.1, 1.0)
    placement = jax.random.permutation(arg_keys[3], EXPERTS).astype(jnp.int32)
    swap_flag = with_ends((jax.random.randint(arg_keys[4], (PAIRS,), 0, 2) < 1).astype(jnp.int32), jax.random.fold_in(arg_keys[4], 1), 0, 1)
    gate_up = noise(arg_keys[5], (EXPERTS, 2, FFN, D), D ** -0.5, 0.09375, ((0, 64), (2, 8)))
    down_weight = noise(arg_keys[6], (EXPERTS, FFN, D), FFN ** -0.5, 0.21875, ((0, 64), (2, 8)))
    return {"tokens": tokens, "expert_ids": expert_ids, "route_weight": route_weight, "placement": placement, "swap_flag": swap_flag, "gate_up": gate_up, "down_weight": down_weight}


def reference(tokens, expert_ids, route_weight, placement, swap_flag, gate_up, down_weight):
    flag_of = swap_flag[placement % PAIRS]
    owner = (placement + PAIRS * flag_of) % EXPERTS
    flat_ids = expert_ids.reshape(-1)
    dest = owner[flat_ids]
    counts = jnp.zeros((EXPERTS,), jnp.int32).at[dest].add(1)
    column_load = counts.astype(jnp.float32) / jnp.float32(TOK_DEV * TOPK)
    slot_range = jnp.arange(EXPERTS, dtype=jnp.int32)
    partner = ((slot_range + PAIRS * swap_flag[slot_range % PAIRS]) % EXPERTS).astype(jnp.int32)
    slot_gate_up = gate_up[partner]
    slot_down = down_weight[partner]
    flat_w = route_weight.reshape(-1)
    tok_of = jnp.arange(TOKENS * TOPK, dtype=jnp.int32) // TOPK
    limit = N_EXPERT * CAP

    def one_expert(total, expert):
        chosen = flat_ids == expert
        order = jnp.cumsum(chosen.astype(jnp.int32)) - 1
        target = jnp.where(chosen, order, limit).astype(jnp.int32)
        rows = jnp.zeros((limit,), jnp.int32).at[target].set(tok_of, mode="drop")
        weights = jnp.zeros((limit,), flat_w.dtype).at[target].set(flat_w, mode="drop")
        slot = placement[expert]
        w_pair = lax.dynamic_index_in_dim(gate_up, slot, 0, keepdims=False).reshape(2 * FFN, D)
        w_down = lax.dynamic_index_in_dim(down_weight, slot, 0, keepdims=False)
        picked = tokens[rows]
        projected = lax.dot_general(picked, w_pair, (((1,), (1,)), ((), ())), preferred_element_type=jnp.float32)
        hidden = (jax.nn.silu(projected[:, :FFN]) * projected[:, FFN:]).astype(jnp.bfloat16)
        result = jnp.dot(hidden, w_down, preferred_element_type=jnp.float32).astype(jnp.bfloat16)
        total = total.at[rows].add(weights[:, None] * result.astype(jnp.float32))
        return total, None

    start = jnp.zeros((TOKENS, D), jnp.float32)
    total, _ = lax.scan(one_expert, start, jnp.arange(EXPERTS, dtype=jnp.int32))
    return total.astype(jnp.bfloat16), column_load, slot_gate_up, slot_down
```

```python
import jax
import jax.numpy as jnp
from jax import lax
from jax.experimental import pallas as pl
from jax.experimental.pallas import tpu as pltpu
from jax.sharding import PartitionSpec as P

MESH = pl.DeviceIdType.MESH
BF = jnp.bfloat16
F32 = jnp.float32
NT = (((1,), (1,)), ((), ()))
TN = (((0,), (0,)), ((), ()))

NE = 64
TOK = 128
FEAT = 512
MAIN, EXT = 16, 4
WIDE = FEAT + 128
UNITS = 96
ROWS = NE * (MAIN + EXT)
TILE = 256


def iota(shape, axis):
    return lax.broadcasted_iota(jnp.int32, shape, axis)


def flag(cond, dtype=BF):
    return jnp.where(cond, 1.0, 0.0).astype(dtype)


def shuffle_matrix():
    row, col = iota((128, 128), 0), iota((128, 128), 1)
    home = ((row % 16) // 4) * 32 + (row // 16) * 4 + row % 4
    return flag(home == col)


def pack(chunk, q):
    tall = jnp.concatenate([chunk[:, 128 * c : 128 * c + 128] for c in range(4)], axis=0)
    return jnp.dot(q, tall, preferred_element_type=F32).astype(BF).reshape(8, 16, 128)


def unpack(packed, q):
    tall = lax.dot_general(q, packed.reshape(128, 128), TN, preferred_element_type=F32).astype(BF)
    return jnp.concatenate([tall[32 * c : 32 * c + 32] for c in range(4)], axis=1)


def kernel(
    tokens, ids, weight, place, gu, down,
    out, totals, got_gu, got_down,
    x_send, x_all, y_send, y_back, ext, w, wd, acc, acc_in, hid, mix,
    s_send, s_recv, x_sems, x_recv, h_send, h_recv, l_sem,
):
    dp, me = lax.axis_index("dp"), lax.axis_index("expert")
    yh, xx = dp // 4, lax.rem(dp, 4)
    ypeer = lax.rem(dp + 4, 8)
    spouse = lax.rem(me + 32, NE)

    barrier = pltpu.get_barrier_semaphore()

    def greet(i, carry):
        pl.semaphore_signal(barrier, inc=1, device_id={"expert": lax.rem(me + i, NE)}, device_id_type=MESH)
        return carry

    lax.fori_loop(1, NE, greet, 0)

    def greet_dp(i, carry):
        pl.semaphore_signal(barrier, inc=1, device_id={"dp": lax.rem(dp + i, 8)}, device_id_type=MESH)
        return carry

    lax.fori_loop(1, 8, greet_dp, 0)

    half = pl.multiple_of(yh * 2048, 2048)
    other = pl.multiple_of((1 - yh) * 2048, 2048)
    local = []
    for g in range(2):
        local.append(pltpu.make_async_copy(gu.at[0, g, :, pl.ds(half, 2048)], w.at[pl.ds(g * UNITS, UNITS)], l_sem.at[g]))
    local.append(pltpu.make_async_copy(down.at[0], wd, l_sem.at[2]))
    for c in local:
        c.start()

    onehot = jnp.zeros((TOK, NE), F32)
    wide_w = jnp.zeros((TOK, NE), F32)
    for k in range(8):
        hit = ids[:, k : k + 1] == iota((TOK, NE), 1)
        onehot = onehot + jnp.where(hit, 1.0, 0.0)
        wide_w = wide_w + jnp.where(hit, weight[:, k : k + 1], 0.0)
    perm = flag(place[...] == iota((NE, 128), 1))
    has = jnp.dot(onehot.astype(BF), perm, preferred_element_type=F32)
    before = flag(iota((TOK, TOK), 1) < iota((TOK, TOK), 0))
    count = jnp.dot(before, has.astype(BF), preferred_element_type=F32)
    pos = jnp.where(has > 0.5, count, -1.0).astype(BF)
    spread_m = flag(iota((128, NE * MAIN), 1) // MAIN == iota((128, NE * MAIN), 0))
    spread_x = flag(iota((128, NE * EXT), 1) // EXT == iota((128, NE * EXT), 0))
    row_m = (iota((TOK, NE * MAIN), 1) % MAIN).astype(F32)
    row_x = (iota((TOK, NE * EXT), 1) % EXT + MAIN).astype(F32)
    at_m = jnp.dot(pos, spread_m, preferred_element_type=F32) == row_m
    at_x = jnp.dot(pos, spread_x, preferred_element_type=F32) == row_x
    q = shuffle_matrix()
    x_send[:, :, :FEAT] = (
        lax.dot_general(flag(at_m), tokens[...], TN, preferred_element_type=F32).astype(BF).reshape(NE, MAIN, FEAT)
    )
    further = lax.dot_general(flag(at_x), tokens[...], TN, preferred_element_type=F32)
    tally = jnp.dot(flag(iota((NE * EXT, TOK), 0) % EXT == 3), has.astype(BF), preferred_element_type=F32)
    ext[:, :128] = (further[:, :128] + tally).astype(BF)
    ext[:, 128:] = further[:, 128:].astype(BF)
    for b in range(8):
        x_send[8 * b : 8 * b + 8, :, FEAT:] = pack(ext[32 * b : 32 * b + 32, :], q)

    pl.semaphore_wait(barrier, NE - 1 + 7)

    def send_rows(n, carry):
        step = (n + 1) // 2
        d = lax.rem(jnp.where(lax.rem(n, 2) == 1, me + step, me + NE - step), NE)
        pltpu.make_async_remote_copy(
            x_send.at[d], x_all.at[xx, me], s_send.at[0], s_recv.at[0], device_id={"expert": d}, device_id_type=MESH
        ).start()
        return carry

    lax.fori_loop(1, NE, send_rows, 0)
    mine = pltpu.make_async_copy(x_send.at[me], x_all.at[xx, me], l_sem.at[3])
    mine.start()
    trade = []
    for g in range(2):
        trade.append(
            pltpu.make_async_remote_copy(
                gu.at[0, g, :, pl.ds(other, 2048)], w.at[pl.ds((2 + g) * UNITS, UNITS)],
                s_send.at[1 + g], s_recv.at[1 + g], device_id={"dp": ypeer}, device_id_type=MESH,
            )
        )
    for c in trade:
        c.start()
    swap = [
        pltpu.make_async_remote_copy(gu, got_gu, s_send.at[3], s_recv.at[3], device_id={"expert": spouse}, device_id_type=MESH),
        pltpu.make_async_remote_copy(down, got_down, s_send.at[4], s_recv.at[4], device_id={"expert": spouse}, device_id_type=MESH),
    ]
    for c in swap:
        c.start()

    rest = wide_w
    for n in range(3):
        term = rest.astype(BF)
        rest = rest - term.astype(F32)
        by_slot = jnp.dot(term, perm, preferred_element_type=F32).astype(BF)
        mix[n, :, : NE * MAIN] = jnp.where(at_m, jnp.dot(by_slot, spread_m, preferred_element_type=F32), 0.0).astype(BF)
        mix[n, :, NE * MAIN :] = jnp.where(at_x, jnp.dot(by_slot, spread_x, preferred_element_type=F32), 0.0).astype(BF)
    acc[...] = jnp.zeros_like(acc)
    for c in local:
        c.wait()

    mine.wait()
    pltpu.make_async_copy(x_all.at[xx, pl.ds(0, NE - 1)], x_all.at[xx, pl.ds(0, NE - 1)], s_recv.at[0]).wait()

    def along_x(i):
        p = yh * 4 + lax.rem(xx + i, 4)
        return pltpu.make_async_remote_copy(
            x_all.at[xx], x_all.at[xx], x_sems.at[i - 1], x_recv.at[i - 1], device_id={"dp": p}, device_id_type=MESH
        )

    around = [along_x(1), along_x(3), along_x(2)]
    for c in around:
        c.start()
    for c in trade:
        c.wait_recv()

    def project(source):
        for b in range(8):
            ext[32 * b : 32 * b + 32, :] = unpack(x_all[source, 8 * b : 8 * b + 8, :, FEAT:], q)
        ww = w[:, pl.ds(pl.multiple_of(source * FEAT, FEAT), FEAT)]

        def tile(t, carry):
            rows = x_all[source, pl.ds(t * 16, 16), :, :FEAT].reshape(TILE, FEAT)
            acc[:, pl.ds(pl.multiple_of(t * TILE, TILE), TILE)] += lax.dot_general(ww, rows, NT, preferred_element_type=F32)
            return carry

        lax.fori_loop(0, 4, tile, 0)
        acc[:, 4 * TILE :] += lax.dot_general(ww, ext[...], NT, preferred_element_type=F32)

    project(xx)
    sel = flag(iota((8, NE * EXT), 1) % EXT == 3)
    totals[...] = jnp.dot(sel, ext[:, :128], preferred_element_type=F32)
    for i, c in ((1, around[0]), (3, around[1]), (2, around[2])):
        c.wait_recv()
        project(lax.rem(xx + 4 - i, 4))

    part = pltpu.make_async_remote_copy(
        acc.at[pl.ds(2 * UNITS, 2 * UNITS)], acc_in, s_send.at[5], s_recv.at[5], device_id={"dp": ypeer}, device_id_type=MESH
    )
    part.start()
    part.wait_recv()
    gate = acc[:UNITS, :] + acc_in[:UNITS, :]
    up = acc[UNITS : 2 * UNITS, :] + acc_in[UNITS:, :]
    here = pl.ds(pl.multiple_of(dp * UNITS, UNITS), UNITS)
    hid[here, :] = (gate / (1.0 + jnp.exp(-gate)) * up).astype(BF)

    def send_hidden(i, carry):
        pltpu.make_async_remote_copy(
            hid.at[here], hid.at[here], h_send, h_recv, device_id={"dp": lax.rem(dp + i, 8)}, device_id_type=MESH
        ).start()
        return carry

    lax.fori_loop(1, 8, send_hidden, 0)
    seven = hid.at[pl.ds(0, 7 * UNITS)]
    pltpu.make_async_copy(seven, seven, h_recv).wait()

    def produce(t):
        part = hid[:, pl.ds(pl.multiple_of(t * TILE, TILE), TILE)]
        return lax.dot_general(part, wd[...], TN, preferred_element_type=F32).astype(BF)

    def result(t, carry):
        y_send[pl.ds(t * 16, 16), :, :FEAT] = produce(t).reshape(16, MAIN, FEAT)
        return carry

    lax.fori_loop(0, 4, result, 0)
    ext[...] = produce(4)
    for b in range(8):
        y_send[8 * b : 8 * b + 8, :, FEAT:] = pack(ext[32 * b : 32 * b + 32, :], q)

    def send_back(n, carry):
        step = (n + 1) // 2
        d = lax.rem(jnp.where(lax.rem(n, 2) == 1, me + step, me + NE - step), NE)
        pltpu.make_async_remote_copy(
            y_send.at[d], y_back.at[me], s_send.at[6], s_recv.at[6], device_id={"expert": d}, device_id_type=MESH
        ).start()
        return carry

    lax.fori_loop(1, NE, send_back, 0)
    own = pltpu.make_async_copy(y_send.at[me], y_back.at[me], l_sem.at[3])
    own.start()
    own.wait()
    many = y_back.at[pl.ds(0, NE - 1)]
    pltpu.make_async_copy(many, many, s_recv.at[6]).wait()

    for b in range(8):
        ext[32 * b : 32 * b + 32, :] = unpack(y_back[8 * b : 8 * b + 8, :, FEAT:], q)
    rows = y_back[:, :, :FEAT].reshape(NE * MAIN, FEAT)
    total = jnp.zeros((TOK, FEAT), F32)
    for n in range(3):
        total = total + jnp.dot(mix[n, :, : NE * MAIN], rows, preferred_element_type=F32)
        total = total + jnp.dot(mix[n, :, NE * MAIN :], ext[...], preferred_element_type=F32)
    out[...] = total.astype(BF)

    sent = x_send.at[pl.ds(0, NE - 1)]
    pltpu.make_async_copy(sent, sent, s_send.at[0]).wait()
    pltpu.make_async_copy(sent, sent, s_send.at[6]).wait()
    pltpu.make_async_copy(seven, seven, h_send).wait()
    part.wait_send()
    for c in trade + around:
        c.wait_send()
    for c in swap:
        c.wait()


def body(tokens, expert_ids, route_weight, placement, swap_flag, gate_up, down_weight):
    vmem = pl.BlockSpec(memory_space=pltpu.VMEM)
    hbm = pl.BlockSpec(memory_space=pl.ANY)
    moe_out, totals, got_gu, got_down = pl.pallas_call(
        kernel,
        out_shape=[
            jax.ShapeDtypeStruct((TOK, FEAT), BF),
            jax.ShapeDtypeStruct((8, 128), F32),
            jax.ShapeDtypeStruct(gate_up.shape, BF),
            jax.ShapeDtypeStruct(down_weight.shape, BF),
        ],
        in_specs=[vmem, vmem, vmem, vmem, hbm, hbm],
        out_specs=[vmem, vmem, hbm, hbm],
        scratch_shapes=[
            pltpu.VMEM((NE, MAIN, WIDE), BF),
            pltpu.VMEM((4, NE, MAIN, WIDE), BF),
            pltpu.VMEM((NE, MAIN, WIDE), BF),
            pltpu.VMEM((NE, MAIN, WIDE), BF),
            pltpu.VMEM((NE * EXT, FEAT), BF),
            pltpu.VMEM((4 * UNITS, 4 * FEAT), BF),
            pltpu.VMEM((8 * UNITS, FEAT), BF),
            pltpu.VMEM((4 * UNITS, ROWS), F32),
            pltpu.VMEM((2 * UNITS, ROWS), F32),
            pltpu.VMEM((8 * UNITS, ROWS), BF),
            pltpu.VMEM((3, TOK, ROWS), BF),
            pltpu.SemaphoreType.DMA((7,)),
            pltpu.SemaphoreType.DMA((7,)),
            pltpu.SemaphoreType.DMA((3,)),
            pltpu.SemaphoreType.DMA((3,)),
            pltpu.SemaphoreType.DMA,
            pltpu.SemaphoreType.DMA,
            pltpu.SemaphoreType.DMA((4,)),
        ],
        compiler_params=pltpu.CompilerParams(
            collective_id=0, has_side_effects=True, vmem_limit_bytes=48 << 20
        ),
        cost_estimate=pl.CostEstimate(flops=5_000_000_000, bytes_accessed=10_000_000, transcendentals=200_000),
        name="experts",
    )(tokens, expert_ids, route_weight, placement.reshape(NE, 1), gate_up, down_weight)
    flags = jnp.concatenate([swap_flag, swap_flag]) == 1
    load = totals[0, :NE]
    column_load = jnp.where(flags, jnp.roll(load, NE // 2), load) / jnp.float32(TOK * 8)
    mine = jnp.arange(NE // 2, dtype=jnp.int32) == lax.axis_index("expert") % (NE // 2)
    swapped = jnp.sum(jnp.where(mine, swap_flag, 0)) == 1
    return (
        moe_out,
        column_load,
        jnp.where(swapped, got_gu, gate_up),
        jnp.where(swapped, got_down, down_weight),
    )


def solution(mesh):
    return jax.shard_map(
        body,
        mesh=mesh,
        in_specs=(
            P("expert", "dp"),
            P("expert", None),
            P("expert", None),
            P(),
            P(),
            P("expert", None, "dp", None),
            P("expert", None, "dp"),
        ),
        out_specs=(P("expert", "dp"), P(), P("expert", None, "dp", None), P("expert", None, "dp")),
        check_vma=False,
    )
```

```python
import jax
import jax.numpy as jnp
from jax import lax
from jax.experimental import pallas as pl
from jax.experimental.pallas import tpu as pltpu
from jax.sharding import PartitionSpec as P

MESH = pl.DeviceIdType.MESH
BF = jnp.bfloat16
F32 = jnp.float32
NN = (((1,), (0,)), ((), ()))
NT = (((1,), (1,)), ((), ()))
TN = (((0,), (0,)), ((), ()))

NE = 64
NZ = 16
TOK = 128
FEAT = 512
MAIN, EXT = 16, 4
WIDE = FEAT + 128
UNITS = 96
TILE = 256
TILES = 5


def iota(shape, axis):
    return lax.broadcasted_iota(jnp.int32, shape, axis)


def flag(cond):
    return jnp.where(cond, 1.0, 0.0).astype(BF)


def dot(a, b, dims=NN):
    return lax.dot_general(a, b, dims, preferred_element_type=F32)


def shuffle8():
    row, col = iota((128, 128), 0), iota((128, 128), 1)
    return flag(((row % 16) // 4) * 32 + (row // 16) * 4 + row % 4 == col)


def shuffle4():
    row, col = iota((64, 64), 0), iota((64, 64), 1)
    return flag(((row % 16) // 4) * 16 + (row // 16) * 4 + row % 4 == col)


def tall(rows):
    return jnp.concatenate([rows[:, 128 * c : 128 * c + 128] for c in range(4)], axis=0)


def broad(rows):
    n = rows.shape[0] // 4
    return jnp.concatenate([rows[n * c : n * c + n] for c in range(4)], axis=1)


def over_rows(values):
    row = iota((16, TOK), 0) // EXT
    last = sum(jnp.where(row == j, values[j], 0.0) for j in range(4))
    return jnp.concatenate([jnp.broadcast_to(v, (MAIN, TOK)) for v in values] + [last], axis=0)


def row_number():
    row = iota((80, TOK), 0)
    return jnp.where(row < 64, row % MAIN, MAIN + row % EXT).astype(F32)


def kernel(
    tokens, ids, weight, place, gu, down,
    out, totals, got_gu, got_down,
    ring, pick, x_all, wf, wd, p_send, p_own, p_in, hid, ext, y_send, y_in, up_out, up_in, dn_out, dn_in,
    snd, rcv, ru, rd, pr, hr, su, sd, loc,
):
    dp, me = lax.axis_index("dp"), lax.axis_index("expert")
    z, col = me // 4, lax.rem(me, 4)
    above, below = {"expert": lax.rem(me + 4, NE)}, {"expert": lax.rem(me + NE - 4, NE)}
    spouse = {"expert": lax.rem(me + 32, NE)}

    def near(i):
        return {"expert": z * 4 + lax.rem(col + i, 4)}

    def peer(i):
        return {"dp": lax.rem(dp + i, 8)}

    def remote(src, dst, send, recv, device):
        return pltpu.make_async_remote_copy(src, dst, send, recv, device_id=device, device_id_type=MESH)

    def await_bytes(ref, sem):
        pltpu.make_async_copy(ref, ref, sem).wait()

    barrier = pltpu.get_barrier_semaphore()
    others = [above, below, spouse] + [near(i) for i in (1, 2, 3)] + [peer(i) for i in range(1, 8)]
    for device in others:
        pl.semaphore_signal(barrier, inc=1, device_id=device, device_id_type=MESH)

    own_units = pl.ds(dp * 2, 2)
    own_feats = pl.ds(pl.multiple_of(dp * FEAT, FEAT), FEAT)
    local = [
        pltpu.make_async_copy(gu.at[0, :, :, own_feats], wf.at[own_units], loc.at[0]),
        pltpu.make_async_copy(down.at[0], wd, loc.at[1]),
    ]
    for c in local:
        c.start()

    lane = iota((TOK, 128), 1)
    place_f = place[...].astype(F32)
    hi = weight[...].astype(BF).astype(F32)
    lo = (weight[...] - hi).astype(BF).astype(F32)
    slots = []
    has = jnp.zeros((TOK, 128), F32)
    facts = jnp.zeros((TOK, 128), F32)
    for k in range(8):
        hit = ids[:, k : k + 1] == iota((TOK, NE), 1)
        slot = jnp.sum(jnp.where(hit, place_f, 0.0), axis=1, keepdims=True)
        slots.append(slot)
        has = has + jnp.where(slot == lane.astype(F32), 1.0, 0.0)
        facts = facts + jnp.where(lane == k, slot, 0.0)
        facts = facts + jnp.where(lane == 16 + k, hi[:, k : k + 1], 0.0) + jnp.where(lane == 24 + k, lo[:, k : k + 1], 0.0)
    before = flag(iota((TOK, TOK), 1) < iota((TOK, TOK), 0))
    count = dot(before, has.astype(BF))
    for k in range(8):
        pos = jnp.sum(jnp.where(slots[k] == lane.astype(F32), count, 0.0), axis=1, keepdims=True)
        facts = facts + jnp.where(lane == 8 + k, pos, 0.0)
    turned = dot(facts.astype(BF), flag(iota((TOK, TOK), 0) == iota((TOK, TOK), 1)), TN).astype(BF)
    ring[z, :TOK, :] = tokens[...]
    ring[z, TOK:, 0:128] = turned[0:16]
    ring[z, TOK:, 128:256] = turned[16:32]
    ring[z, TOK:, 256:384] = jnp.zeros((16, 128), BF)
    ring[z, TOK:, 384:512] = dot(flag(iota((16, TOK), 0) == 0), has.astype(BF)).astype(BF)

    pl.semaphore_wait(barrier, len(others))

    def pass_up(block, s):
        remote(ring.at[block], ring.at[block], snd.at[0], ru.at[s], above).start()

    def pass_down(block, s):
        remote(ring.at[block], ring.at[block], snd.at[1], rd.at[s], below).start()

    pass_up(z, 0)
    pass_down(z, 0)

    def send_weights(i, carry):
        p = lax.rem(dp + i, 8)
        feats = pl.ds(pl.multiple_of(p * FEAT, FEAT), FEAT)
        remote(gu.at[0, :, :, feats], wf.at[own_units], snd.at[3], rcv.at[1], {"dp": p}).start()
        return carry

    lax.fori_loop(1, 8, send_weights, 0)
    swap = [
        remote(gu, got_gu, snd.at[9], rcv.at[3], spouse),
        remote(down, got_down, snd.at[10], rcv.at[4], spouse),
    ]
    for c in swap:
        c.start()

    def by_slot(facts, values):
        return [
            jnp.sum(jnp.where(facts == (z * 4 + j).astype(F32), values, 0.0), axis=0, keepdims=True) for j in range(4)
        ]

    def picked(block):
        facts = ring[block, TOK:, 0:128].astype(F32)
        slot = facts[0:8]
        places = [v - 1.0 for v in by_slot(slot, facts[8:16] + 1.0)]
        return slot, over_rows(places) == row_number()

    def choose(block):
        rows = dot(flag(picked(block)[1]), ring[block, :TOK, :])
        more = rows[64:]
        third = flag((iota((16, 16), 0) % EXT == 3) & (iota((16, 16), 1) == 0))
        tally = dot(third, ring[block, TOK:, 384:512])
        more = tall(jnp.concatenate([more[:, :128] + tally, more[:, 128:]], axis=1)).astype(BF)
        pick[:, block, :, :FEAT] = rows[:64].astype(BF).reshape(4, MAIN, FEAT)
        pick[:, block, :, FEAT:] = dot(shuffle4(), more).astype(BF).reshape(4, MAIN, 128)
        to = col * NZ + block
        for i in (1, 2, 3):
            j = lax.rem(col + i, 4)
            remote(pick.at[j, block], x_all.at[to], snd.at[2], rcv.at[0], near(i)).start()
        pltpu.make_async_copy(pick.at[col, block], x_all.at[to], loc.at[2]).start()

    choose(z)

    def around(s, carry):
        low, high = lax.rem(z + 15 - s, NZ), lax.rem(z + 1 + s, NZ)
        await_bytes(ring.at[low], ru.at[s])
        pass_up(low, s + 1)
        await_bytes(ring.at[high], rd.at[s])

        @pl.when(s < 6)
        def _():
            pass_down(high, s + 1)

        choose(low)
        choose(high)
        return carry

    lax.fori_loop(0, 7, around, 0)
    far = lax.rem(z + 8, NZ)
    await_bytes(ring.at[far], ru.at[7])
    choose(far)

    for c in local:
        c.wait()
    await_bytes(wf.at[pl.ds(0, 14)], rcv.at[1])
    await_bytes(x_all.at[pl.ds(0, 48)], rcv.at[0])
    await_bytes(x_all.at[pl.ds(0, 16)], loc.at[2])

    q8 = shuffle8()
    for b in range(8):
        packed = x_all[8 * b : 8 * b + 8, :, FEAT:].reshape(128, 128)
        ext[32 * b : 32 * b + 32, :] = broad(dot(q8, packed, TN).astype(BF))
    totals[...] = dot(flag(iota((8, NE * EXT), 1) % EXT == 3), ext[:, :128])

    def project(t, rows):
        def one(i, carry):
            p = lax.rem(dp + i, 8)
            p_send[p, t] = dot(wf[pl.ds(p * 2, 2)].reshape(2 * UNITS, FEAT), rows, NT).astype(BF)
            remote(p_send.at[p, t], p_in.at[dp, t], snd.at[4], pr.at[t], {"dp": p}).start()
            return carry

        lax.fori_loop(1, 8, one, 0)
        p_own[t] = dot(wf[own_units].reshape(2 * UNITS, FEAT), rows, NT)

    def project_tile(t, carry):
        project(t, x_all[pl.ds(t * 16, 16), :, :FEAT].reshape(TILE, FEAT))
        return carry

    project(4, ext[...])
    lax.fori_loop(0, 4, project_tile, 0)

    def activate(n, carry):
        t = lax.rem(n + 4, TILES)
        await_bytes(p_in.at[pl.ds(0, 7), t], pr.at[t])
        both = p_own[t]
        for i in range(1, 8):
            both = both + p_in[lax.rem(dp + i, 8), t].astype(F32)
        gate, up = both[:UNITS], both[UNITS:]
        hid[t, dp] = (gate / (1.0 + jnp.exp(-gate)) * up).astype(BF)
        for i in range(1, 8):
            remote(hid.at[t, dp], hid.at[t, dp], snd.at[5], hr.at[t], peer(i)).start()
        return carry

    lax.fori_loop(0, TILES, activate, 0)

    def produce(t):
        await_bytes(hid.at[t, pl.ds(0, 7)], hr.at[t])
        return dot(hid[t].reshape(8 * UNITS, TILE), wd[...], TN).astype(BF)

    ext[...] = produce(4)

    def finish(j):
        rows = pl.ds(j * 16, 16)
        y_send[rows, :, :FEAT] = produce(j).reshape(16, MAIN, FEAT)
        for g in range(2):
            more = tall(ext[pl.ds(pl.multiple_of(j * 64 + g * 32, 32), 32), :])
            y_send[pl.ds(j * 16 + g * 8, 8), :, FEAT:] = dot(q8, more).astype(BF).reshape(8, MAIN, 128)
        return y_send.at[rows]

    def give_back(i, carry):
        ref = finish(lax.rem(col + i, 4))
        remote(ref, y_in.at[col], snd.at[6], rcv.at[2], near(i)).start()
        return carry

    lax.fori_loop(1, 4, give_back, 0)
    mine = pltpu.make_async_copy(finish(col), y_in.at[col], loc.at[3])
    mine.start()
    await_bytes(y_in.at[pl.ds(0, 3)], rcv.at[2])
    mine.wait()

    def combine(block):
        slot, at = picked(block)
        terms = ring[block, TOK:, 128:256].astype(F32)
        more = broad(dot(shuffle4(), y_in[:, block, :, FEAT:].reshape(64, 128), TN).astype(BF))
        rows = jnp.concatenate([y_in[:, block, :, :FEAT].reshape(64, FEAT), more], axis=0)
        share = jnp.zeros((TOK, FEAT), F32)
        for n in range(2):
            mix = jnp.where(at, over_rows(by_slot(slot, terms[8 * n : 8 * n + 8])), 0.0)
            share = share + dot(mix.astype(BF), rows, TN)
        return share

    def hand_up(s, total):
        up_out[s] = total.astype(BF)
        remote(up_out.at[s], up_in.at[s], snd.at[7], su.at[s], above).start()

    def hand_down(s, total):
        dn_out[s] = total.astype(BF)
        remote(dn_out.at[s], dn_in.at[s], snd.at[8], sd.at[s], below).start()

    hand_up(0, combine(far))
    hand_down(0, combine(lax.rem(z + 9, NZ)))

    def home(s, carry):
        share = combine(lax.rem(z + 8 - s, NZ))
        await_bytes(up_in.at[s - 1], su.at[s - 1])
        hand_up(s, share + up_in[s - 1].astype(F32))
        share = combine(lax.rem(z + 9 + s, NZ))
        await_bytes(dn_in.at[s - 1], sd.at[s - 1])
        hand_down(s, share + dn_in[s - 1].astype(F32))
        return carry

    lax.fori_loop(1, 7, home, 0)
    share = combine(lax.rem(z + 1, NZ))
    await_bytes(up_in.at[6], su.at[6])
    hand_up(7, share + up_in[6].astype(F32))
    share = combine(z)
    await_bytes(dn_in.at[6], sd.at[6])
    share = share + dn_in[6].astype(F32)
    await_bytes(up_in.at[7], su.at[7])
    out[...] = (share + up_in[7].astype(F32)).astype(BF)

    await_bytes(ring.at[pl.ds(0, 8)], snd.at[0])
    await_bytes(ring.at[pl.ds(0, 7)], snd.at[1])
    await_bytes(x_all.at[pl.ds(0, 48)], snd.at[2])
    await_bytes(wf.at[pl.ds(0, 14)], snd.at[3])
    await_bytes(p_in.at[pl.ds(0, 7)], snd.at[4])
    await_bytes(hid.at[:, pl.ds(0, 7)], snd.at[5])
    await_bytes(y_in.at[pl.ds(0, 3)], snd.at[6])
    await_bytes(up_out, snd.at[7])
    await_bytes(dn_out, snd.at[8])
    for c in swap:
        c.wait()


def body(tokens, expert_ids, route_weight, placement, swap_flag, gate_up, down_weight):
    vmem = pl.BlockSpec(memory_space=pltpu.VMEM)
    hbm = pl.BlockSpec(memory_space=pl.ANY)
    moe_out, totals, got_gu, got_down = pl.pallas_call(
        kernel,
        out_shape=[
            jax.ShapeDtypeStruct((TOK, FEAT), BF),
            jax.ShapeDtypeStruct((8, 128), F32),
            jax.ShapeDtypeStruct(gate_up.shape, BF),
            jax.ShapeDtypeStruct(down_weight.shape, BF),
        ],
        in_specs=[vmem, vmem, vmem, vmem, hbm, hbm],
        out_specs=[vmem, vmem, hbm, hbm],
        scratch_shapes=[
            pltpu.VMEM((NZ, TOK + 16, FEAT), BF),
            pltpu.VMEM((4, NZ, MAIN, WIDE), BF),
            pltpu.VMEM((NE, MAIN, WIDE), BF),
            pltpu.VMEM((16, UNITS, FEAT), BF),
            pltpu.VMEM((8 * UNITS, FEAT), BF),
            pltpu.VMEM((8, TILES, 2 * UNITS, TILE), BF),
            pltpu.VMEM((TILES, 2 * UNITS, TILE), F32),
            pltpu.VMEM((8, TILES, 2 * UNITS, TILE), BF),
            pltpu.VMEM((TILES, 8, UNITS, TILE), BF),
            pltpu.VMEM((NE * EXT, FEAT), BF),
            pltpu.VMEM((NE, MAIN, WIDE), BF),
            pltpu.VMEM((4, NZ, MAIN, WIDE), BF),
            pltpu.VMEM((8, TOK, FEAT), BF),
            pltpu.VMEM((8, TOK, FEAT), BF),
            pltpu.VMEM((7, TOK, FEAT), BF),
            pltpu.VMEM((7, TOK, FEAT), BF),
            pltpu.SemaphoreType.DMA((11,)),
            pltpu.SemaphoreType.DMA((5,)),
            pltpu.SemaphoreType.DMA((8,)),
            pltpu.SemaphoreType.DMA((7,)),
            pltpu.SemaphoreType.DMA((TILES,)),
            pltpu.SemaphoreType.DMA((TILES,)),
            pltpu.SemaphoreType.DMA((8,)),
            pltpu.SemaphoreType.DMA((7,)),
            pltpu.SemaphoreType.DMA((4,)),
        ],
        compiler_params=pltpu.CompilerParams(
            collective_id=0, has_side_effects=True, vmem_limit_bytes=48 << 20
        ),
        cost_estimate=pl.CostEstimate(flops=5_000_000_000, bytes_accessed=10_000_000, transcendentals=200_000),
        name="experts",
    )(tokens, expert_ids, route_weight, placement.reshape(1, NE), gate_up, down_weight)
    flags = jnp.concatenate([swap_flag, swap_flag]) == 1
    load = totals[0, :NE]
    column_load = jnp.where(flags, jnp.roll(load, NE // 2), load) / jnp.float32(TOK * 8)
    mine = jnp.arange(NE // 2, dtype=jnp.int32) == lax.axis_index("expert") % (NE // 2)
    swapped = jnp.sum(jnp.where(mine, swap_flag, 0)) == 1
    return (
        moe_out,
        column_load,
        jnp.where(swapped, got_gu, gate_up),
        jnp.where(swapped, got_down, down_weight),
    )


def solution(mesh):
    return jax.shard_map(
        body,
        mesh=mesh,
        in_specs=(
            P("expert", "dp"),
            P("expert", None),
            P("expert", None),
            P(),
            P(),
            P("expert", None, "dp", None),
            P("expert", None, "dp"),
        ),
        out_specs=(P("expert", "dp"), P(), P("expert", None, "dp", None), P("expert", None, "dp")),
        check_vma=False,
    )
```

```python
import functools

import jax
import jax.numpy as jnp
from jax import lax
from jax.experimental import pallas as pl
from jax.experimental.pallas import tpu as pltpu
from jax.sharding import PartitionSpec as P

MESH = pl.DeviceIdType.MESH
BF = jnp.bfloat16
F32 = jnp.float32
NN = (((1,), (0,)), ((), ()))
NT = (((1,), (1,)), ((), ()))
TN = (((0,), (0,)), ((), ()))

NE = 64
NZ = 16
TOK = 128
FEAT = 512
MAIN, EXT = 16, 4
WIDE = FEAT + 128
UNITS = 96
TILE = 256
TILES = 5


def iota(shape, axis):
    return lax.broadcasted_iota(jnp.int32, shape, axis)


def flag(cond):
    return jnp.where(cond, 1.0, 0.0).astype(BF)


def dot(a, b, dims=NN):
    return lax.dot_general(a, b, dims, preferred_element_type=F32)


def shuffle8():
    row, col = iota((128, 128), 0), iota((128, 128), 1)
    return flag(((row % 16) // 4) * 32 + (row // 16) * 4 + row % 4 == col)


def shuffle4():
    row, col = iota((64, 64), 0), iota((64, 64), 1)
    return flag(((row % 16) // 4) * 16 + (row // 16) * 4 + row % 4 == col)


def tall(rows):
    return jnp.concatenate([rows[:, 128 * c : 128 * c + 128] for c in range(4)], axis=0)


def broad(rows):
    n = rows.shape[0] // 4
    return jnp.concatenate([rows[n * c : n * c + n] for c in range(4)], axis=1)


def over_rows(values):
    row = iota((16, TOK), 0) // EXT
    last = sum(jnp.where(row == j, values[j], 0.0) for j in range(4))
    return jnp.concatenate([jnp.broadcast_to(v, (MAIN, TOK)) for v in values] + [last], axis=0)


def row_number():
    row = iota((80, TOK), 0)
    return jnp.where(row < 64, row % MAIN, MAIN + row % EXT).astype(F32)


def kernel(
    tokens, ids, weight, place, gu, down,
    out, totals, got_gu,
    ring, pick, x_all, w, wd, p_send, p_own, p_in, hid, ext, y_send, y_in, up_out, up_in, dn_out, dn_in,
    snd, rcv, ru, rd, pr, hr, su, sd, loc,
):
    dp, me = lax.axis_index("dp"), lax.axis_index("expert")
    z, col = me // 4, lax.rem(me, 4)
    above, below = {"expert": lax.rem(me + 4, NE)}, {"expert": lax.rem(me + NE - 4, NE)}
    spouse = {"expert": lax.rem(me + 32, NE)}

    yh, xx = dp // 4, lax.rem(dp, 4)
    across = {"dp": lax.rem(dp + 4, 8)}

    def near(i, k=0):
        return {"dp": yh * 4 + lax.rem(xx + k, 4), "expert": z * 4 + lax.rem(col + i, 4)}

    def peer(i):
        return {"dp": lax.rem(dp + i, 8)}

    def remote(src, dst, send, recv, device):
        return pltpu.make_async_remote_copy(src, dst, send, recv, device_id=device, device_id_type=MESH)

    def await_bytes(ref, sem):
        pltpu.make_async_copy(ref, ref, sem).wait()

    barrier = pltpu.get_barrier_semaphore()
    others = [above, below, spouse] + [near(n % 4, n // 4) for n in range(1, 16)]
    others += [{"dp": (1 - yh) * 4 + lax.rem(xx + k, 4)} for k in range(4)]
    for device in others:
        pl.semaphore_signal(barrier, inc=1, device_id=device, device_id_type=MESH)

    half = pl.ds(pl.multiple_of(yh * 2048, 2048), 2048)
    other_half = pl.ds(pl.multiple_of((1 - yh) * 2048, 2048), 2048)
    local = [
        pltpu.make_async_copy(gu.at[0, :, :, half], w.at[pl.ds(0, 2)], loc.at[0]),
        pltpu.make_async_copy(down.at[0], wd, loc.at[1]),
    ]
    for c in local:
        c.start()

    lane = iota((TOK, 128), 1)
    place_f = place[...].astype(F32)
    hi = weight[...].astype(BF).astype(F32)
    lo = (weight[...] - hi).astype(BF).astype(F32)
    slots = []
    has = jnp.zeros((TOK, 128), F32)
    facts = jnp.zeros((TOK, 128), F32)
    for k in range(8):
        hit = ids[:, k : k + 1] == iota((TOK, NE), 1)
        slot = jnp.sum(jnp.where(hit, place_f, 0.0), axis=1, keepdims=True)
        slots.append(slot)
        has = has + jnp.where(slot == lane.astype(F32), 1.0, 0.0)
        facts = facts + jnp.where(lane == k, slot, 0.0)
        facts = facts + jnp.where(lane == 16 + k, hi[:, k : k + 1], 0.0) + jnp.where(lane == 24 + k, lo[:, k : k + 1], 0.0)
    before = flag(iota((TOK, TOK), 1) < iota((TOK, TOK), 0))
    count = dot(before, has.astype(BF))
    for k in range(8):
        pos = jnp.sum(jnp.where(slots[k] == lane.astype(F32), count, 0.0), axis=1, keepdims=True)
        facts = facts + jnp.where(lane == 8 + k, pos, 0.0)
    turned = dot(facts.astype(BF), flag(iota((TOK, TOK), 0) == iota((TOK, TOK), 1)), TN).astype(BF)
    ring[z, :TOK, :] = tokens[...]
    ring[z, TOK:, 0:128] = turned[0:16]
    ring[z, TOK:, 128:256] = turned[16:32]
    ring[z, TOK:, 256:384] = jnp.zeros((16, 128), BF)
    early = remote(gu.at[0, 0], got_gu.at[0, 0], snd.at[9], rcv.at[3], spouse)
    ring[z, TOK:, 384:512] = dot(flag(iota((16, TOK), 0) == 0), has.astype(BF)).astype(BF)

    pl.semaphore_wait(barrier, len(others))

    def pass_up(block, s):
        remote(ring.at[block], ring.at[block], snd.at[0], ru.at[s], above).start()

    def pass_down(block, s):
        remote(ring.at[block], ring.at[block], snd.at[1], rd.at[s], below).start()

    pass_up(z, 0)
    pass_down(z, 0)

    trade = remote(gu.at[0, :, :, other_half], w.at[pl.ds(2, 2)], snd.at[3], rcv.at[1], across)
    trade.start()

    def by_slot(facts, values):
        return [
            jnp.sum(jnp.where(facts == (z * 4 + j).astype(F32), values, 0.0), axis=0, keepdims=True) for j in range(4)
        ]

    def picked(block):
        facts = ring[block, TOK:, 0:128].astype(F32)
        slot = facts[0:8]
        places = [v - 1.0 for v in by_slot(slot, facts[8:16] + 1.0)]
        return slot, over_rows(places) == row_number()

    def choose(block, n):
        rows = dot(flag(picked(block)[1]), ring[block, :TOK, :])
        more = rows[64:]
        third = flag((iota((16, 16), 0) % EXT == 3) & (iota((16, 16), 1) == 0))
        tally = dot(third, ring[block, TOK:, 384:512])
        more = tall(jnp.concatenate([more[:, :128] + tally, more[:, 128:]], axis=1)).astype(BF)
        pick[:, n, :, :FEAT] = rows[:64].astype(BF).reshape(4, MAIN, FEAT)
        pick[:, n, :, FEAT:] = dot(shuffle4(), more).astype(BF).reshape(4, MAIN, 128)

    def deal(n, blocks):
        src, dst = pl.ds(n, blocks), pl.ds(xx * NE + col * NZ + n, blocks)
        for m in range(1, 16):
            i, k = m % 4, m // 4
            j = lax.rem(col + i, 4)
            remote(pick.at[j, src], x_all.at[dst], snd.at[2], rcv.at[0], near(i, k)).start()
        pltpu.make_async_copy(pick.at[col, src], x_all.at[dst], loc.at[2]).start()

    choose(z, 0)
    deal(0, 1)

    def around(s, carry):
        low, high = lax.rem(z + 15 - s, NZ), lax.rem(z + 1 + s, NZ)
        await_bytes(ring.at[low], ru.at[s])
        pass_up(low, s + 1)
        await_bytes(ring.at[high], rd.at[s])

        @pl.when(s < 6)
        def _():
            pass_down(high, s + 1)

        choose(low, 2 * s + 1)
        choose(high, 2 * s + 2)
        deal(2 * s + 1, 2)
        return carry

    lax.fori_loop(0, 7, around, 0)
    far = lax.rem(z + 8, NZ)
    await_bytes(ring.at[far], ru.at[7])
    choose(far, 15)
    deal(15, 1)

    for c in local:
        c.wait()
    trade.wait_recv()
    await_bytes(x_all.at[pl.ds(0, 15 * NZ)], rcv.at[0])
    await_bytes(x_all.at[pl.ds(0, NZ)], loc.at[2])
    early.start()

    q8 = shuffle8()

    def project(t, rows_of):
        total = jnp.zeros((4 * UNITS, TILE), F32)
        for x in range(4):
            part = w[:, :, x * FEAT : x * FEAT + FEAT].reshape(4 * UNITS, FEAT)
            total = total + dot(part, rows_of(x), NT)
        p_own[t] = total[: 2 * UNITS]
        p_send[t] = total[2 * UNITS :]
        remote(p_send.at[t], p_in.at[t], snd.at[4], pr.at[t], across).start()

    def further_rows(x):
        for b in range(8):
            packed = x_all[x * NE + 8 * b : x * NE + 8 * b + 8, :, FEAT:].reshape(128, 128)
            ext[32 * b : 32 * b + 32, :] = broad(dot(q8, packed, TN).astype(BF))
        if x == 0:
            totals[...] = dot(flag(iota((8, NE * EXT), 1) % EXT == 3), ext[:, :128])
        return ext[...]

    def project_tile(t, carry):
        project(t, lambda x: x_all[pl.ds(x * NE + t * 16, 16), :, :FEAT].reshape(TILE, FEAT))
        return carry

    project(4, further_rows)
    lax.fori_loop(0, 4, project_tile, 0)

    def activate(n, carry):
        t = lax.rem(n + 4, TILES)
        await_bytes(p_in.at[t], pr.at[t])
        both = p_own[t] + p_in[t]
        gate, up = both[:UNITS], both[UNITS:]
        hid[t, dp] = (gate / (1.0 + jnp.exp(-gate)) * up).astype(BF)
        for i in range(1, 8):
            remote(hid.at[t, dp], hid.at[t, dp], snd.at[5], hr.at[t], peer(i)).start()
        return carry

    lax.fori_loop(0, TILES, activate, 0)

    def produce(t):
        await_bytes(hid.at[t, pl.ds(0, 7)], hr.at[t])
        return dot(hid[t].reshape(8 * UNITS, TILE), wd[...], TN).astype(BF)

    ext[...] = produce(4)

    def finish(j):
        rows = pl.ds(j * 16, 16)
        y_send[rows, :, :FEAT] = produce(j).reshape(16, MAIN, FEAT)
        for g in range(2):
            more = tall(ext[pl.ds(pl.multiple_of(j * 64 + g * 32, 32), 32), :])
            y_send[pl.ds(j * 16 + g * 8, 8), :, FEAT:] = dot(q8, more).astype(BF).reshape(8, MAIN, 128)
        return y_send.at[rows]

    def give_back(i, carry):
        ref = finish(lax.rem(col + i, 4))
        remote(ref, y_in.at[col], snd.at[6], rcv.at[2], near(i)).start()
        return carry

    lax.fori_loop(1, 4, give_back, 0)
    mine = pltpu.make_async_copy(finish(col), y_in.at[col], loc.at[3])
    mine.start()
    await_bytes(y_in.at[pl.ds(0, 3)], rcv.at[2])
    mine.wait()

    def combine(block, n):
        slot, at = picked(block)
        terms = ring[block, TOK:, 128:256].astype(F32)
        more = broad(dot(shuffle4(), y_in[:, n, :, FEAT:].reshape(64, 128), TN).astype(BF))
        rows = jnp.concatenate([y_in[:, n, :, :FEAT].reshape(64, FEAT), more], axis=0)
        share = jnp.zeros((TOK, FEAT), F32)
        for part in range(2):
            mix = jnp.where(at, over_rows(by_slot(slot, terms[8 * part : 8 * part + 8])), 0.0)
            share = share + dot(mix.astype(BF), rows, TN)
        return share

    def hand_up(s, total):
        up_out[s] = total.astype(BF)
        remote(up_out.at[s], up_in.at[s], snd.at[7], su.at[s], above).start()

    def hand_down(s, total):
        dn_out[s] = total.astype(BF)
        remote(dn_out.at[s], dn_in.at[s], snd.at[8], sd.at[s], below).start()

    hand_up(0, combine(far, 15))
    hand_down(0, combine(lax.rem(z + 9, NZ), 13))

    def home(s, carry):
        share = combine(lax.rem(z + 8 - s, NZ), 16 - 2 * s)
        await_bytes(up_in.at[s - 1], su.at[s - 1])
        hand_up(s, share + up_in[s - 1].astype(F32))
        share = combine(lax.rem(z + 9 + s, NZ), 13 - 2 * s)
        await_bytes(dn_in.at[s - 1], sd.at[s - 1])
        hand_down(s, share + dn_in[s - 1].astype(F32))
        return carry

    lax.fori_loop(1, 7, home, 0)
    share = combine(lax.rem(z + 1, NZ), 2)
    await_bytes(up_in.at[6], su.at[6])
    hand_up(7, share + up_in[6].astype(F32))
    share = combine(z, 0)
    await_bytes(dn_in.at[6], sd.at[6])
    share = share + dn_in[6].astype(F32)
    await_bytes(up_in.at[7], su.at[7])
    out[...] = (share + up_in[7].astype(F32)).astype(BF)

    await_bytes(ring.at[pl.ds(0, 8)], snd.at[0])
    await_bytes(ring.at[pl.ds(0, 7)], snd.at[1])
    await_bytes(x_all.at[pl.ds(0, 15 * NZ)], snd.at[2])
    trade.wait_send()
    await_bytes(p_in, snd.at[4])
    await_bytes(hid.at[:, pl.ds(0, 7)], snd.at[5])
    await_bytes(y_in.at[pl.ds(0, 3)], snd.at[6])
    await_bytes(up_out, snd.at[7])
    await_bytes(dn_out, snd.at[8])
    early.wait()


def exchange_kernel(pair, gu, down, old_gu, old_down, got_gu, got_down, snd, rcv):
    me = lax.axis_index("expert")
    spouse = {"expert": lax.rem(me + NE // 2, NE)}

    @pl.when(lax.rem(me, NE // 2) == pair)
    def _():
        barrier = pltpu.get_barrier_semaphore()
        pl.semaphore_signal(barrier, inc=1, device_id=spouse, device_id_type=MESH)
        pl.semaphore_wait(barrier, 1)
        copies = [
            pltpu.make_async_remote_copy(src, dst, snd.at[n], rcv.at[n], device_id=spouse, device_id_type=MESH)
            for n, (src, dst) in enumerate([(gu.at[0, 1], got_gu.at[0, 1]), (down, got_down)])
        ]
        for c in copies:
            c.start()
        for c in copies:
            c.wait()


def exchange(pair, gu, down, old_gu, old_down):
    hbm = pl.BlockSpec(memory_space=pl.ANY)
    return tuple(
        pl.pallas_call(
            functools.partial(exchange_kernel, pair),
            out_shape=[jax.ShapeDtypeStruct(old_gu.shape, BF), jax.ShapeDtypeStruct(old_down.shape, BF)],
            in_specs=[hbm] * 4,
            out_specs=[hbm] * 2,
            input_output_aliases={2: 0, 3: 1},
            scratch_shapes=[pltpu.SemaphoreType.DMA((2,)), pltpu.SemaphoreType.DMA((2,))],
            compiler_params=pltpu.CompilerParams(collective_id=1 + pair, has_side_effects=True),
            name="exchange",
        )(gu, down, old_gu, old_down)
    )


def body(tokens, expert_ids, route_weight, placement, swap_flag, gate_up, down_weight):
    vmem = pl.BlockSpec(memory_space=pltpu.VMEM)
    hbm = pl.BlockSpec(memory_space=pl.ANY)
    moe_out, totals, got_gu = pl.pallas_call(
        kernel,
        out_shape=[
            jax.ShapeDtypeStruct((TOK, FEAT), BF),
            jax.ShapeDtypeStruct((8, 128), F32),
            jax.ShapeDtypeStruct(gate_up.shape, BF),
        ],
        in_specs=[vmem, vmem, vmem, vmem, hbm, hbm],
        out_specs=[vmem, vmem, hbm],
        scratch_shapes=[
            pltpu.VMEM((NZ, TOK + 16, FEAT), BF),
            pltpu.VMEM((4, NZ, MAIN, WIDE), BF),
            pltpu.VMEM((4 * NE, MAIN, WIDE), BF),
            pltpu.VMEM((4, UNITS, 4 * FEAT), BF),
            pltpu.VMEM((8 * UNITS, FEAT), BF),
            pltpu.VMEM((TILES, 2 * UNITS, TILE), F32),
            pltpu.VMEM((TILES, 2 * UNITS, TILE), F32),
            pltpu.VMEM((TILES, 2 * UNITS, TILE), F32),
            pltpu.VMEM((TILES, 8, UNITS, TILE), BF),
            pltpu.VMEM((NE * EXT, FEAT), BF),
            pltpu.VMEM((NE, MAIN, WIDE), BF),
            pltpu.VMEM((4, NZ, MAIN, WIDE), BF),
            pltpu.VMEM((8, TOK, FEAT), BF),
            pltpu.VMEM((8, TOK, FEAT), BF),
            pltpu.VMEM((7, TOK, FEAT), BF),
            pltpu.VMEM((7, TOK, FEAT), BF),
            pltpu.SemaphoreType.DMA((10,)),
            pltpu.SemaphoreType.DMA((4,)),
            pltpu.SemaphoreType.DMA((8,)),
            pltpu.SemaphoreType.DMA((7,)),
            pltpu.SemaphoreType.DMA((TILES,)),
            pltpu.SemaphoreType.DMA((TILES,)),
            pltpu.SemaphoreType.DMA((8,)),
            pltpu.SemaphoreType.DMA((7,)),
            pltpu.SemaphoreType.DMA((4,)),
        ],
        compiler_params=pltpu.CompilerParams(
            collective_id=0, has_side_effects=True, vmem_limit_bytes=48 << 20
        ),
        cost_estimate=pl.CostEstimate(flops=5_000_000_000, bytes_accessed=10_000_000, transcendentals=200_000),
        name="experts",
    )(tokens, expert_ids, route_weight, placement.reshape(1, NE), gate_up, down_weight)
    got = (got_gu, down_weight)
    for pair in range(NE // 2):
        got = lax.cond(
            swap_flag[pair] == 1,
            functools.partial(exchange, pair),
            lambda gu, down, got_gu, got_down: (got_gu, got_down),
            gate_up, down_weight, *got,
        )
    got_gu, got_down = got
    flags = jnp.concatenate([swap_flag, swap_flag]) == 1
    load = totals[0, :NE]
    column_load = jnp.where(flags, jnp.roll(load, NE // 2), load) / jnp.float32(TOK * 8)
    mine = jnp.arange(NE // 2, dtype=jnp.int32) == lax.axis_index("expert") % (NE // 2)
    swapped = jnp.sum(jnp.where(mine, swap_flag, 0)) == 1
    return (
        moe_out,
        column_load,
        jnp.where(swapped, got_gu, gate_up),
        got_down,
    )


def solution(mesh):
    return jax.shard_map(
        body,
        mesh=mesh,
        in_specs=(
            P("expert", "dp"),
            P("expert", None),
            P("expert", None),
            P(),
            P(),
            P("expert", None, "dp", None),
            P("expert", None, "dp"),
        ),
        out_specs=(P("expert", "dp"), P(), P("expert", None, "dp", None), P("expert", None, "dp")),
        check_vma=False,
    )
```

```python
import functools

import jax
import jax.numpy as jnp
from jax import lax
from jax.experimental import pallas as pl
from jax.experimental.pallas import tpu as pltpu
from jax.sharding import PartitionSpec as P

MESH = pl.DeviceIdType.MESH
BF = jnp.bfloat16
F32 = jnp.float32
NN = (((1,), (0,)), ((), ()))
NT = (((1,), (1,)), ((), ()))
TN = (((0,), (0,)), ((), ()))

NE = 64
NZ = 16
TOK = 128
FEAT = 512
MAIN, EXT = 16, 4
WIDE = FEAT + 128
UNITS = 96
TILE = 256
TILES = 5


def iota(shape, axis):
    return lax.broadcasted_iota(jnp.int32, shape, axis)


def flag(cond):
    return jnp.where(cond, 1.0, 0.0).astype(BF)


def dot(a, b, dims=NN):
    return lax.dot_general(a, b, dims, preferred_element_type=F32)


def shuffle8():
    row, col = iota((128, 128), 0), iota((128, 128), 1)
    return flag(((row % 16) // 4) * 32 + (row // 16) * 4 + row % 4 == col)


def shuffle4():
    row, col = iota((64, 64), 0), iota((64, 64), 1)
    return flag(((row % 16) // 4) * 16 + (row // 16) * 4 + row % 4 == col)


def tall(rows):
    return jnp.concatenate([rows[:, 128 * c : 128 * c + 128] for c in range(4)], axis=0)


def broad(rows):
    n = rows.shape[0] // 4
    return jnp.concatenate([rows[n * c : n * c + n] for c in range(4)], axis=1)


def over_rows(values):
    row = iota((16, TOK), 0) // EXT
    last = sum(jnp.where(row == j, values[j], 0.0) for j in range(4))
    return jnp.concatenate([jnp.broadcast_to(v, (MAIN, TOK)) for v in values] + [last], axis=0)


def row_number():
    row = iota((80, TOK), 0)
    return jnp.where(row < 64, row % MAIN, MAIN + row % EXT).astype(F32)


def kernel(
    tokens, ids, weight, place, gu, down,
    out, totals, got_gu, got_down,
    ring, pick, x_all, w, wd, p_send, p_own, p_in, hid, ext, y_send, y_in, up_out, up_in, dn_out, dn_in,
    snd, rcv, ru, rd, pr, hr, su, sd, loc,
):
    dp, me = lax.axis_index("dp"), lax.axis_index("expert")
    z, col = me // 4, lax.rem(me, 4)
    above, below = {"expert": lax.rem(me + 4, NE)}, {"expert": lax.rem(me + NE - 4, NE)}
    spouse = {"expert": lax.rem(me + 32, NE)}

    yh, xx = dp // 4, lax.rem(dp, 4)
    across = {"dp": lax.rem(dp + 4, 8)}

    def near(i, k=0):
        return {"dp": yh * 4 + lax.rem(xx + k, 4), "expert": z * 4 + lax.rem(col + i, 4)}

    def peer(i):
        return {"dp": lax.rem(dp + i, 8)}

    def remote(src, dst, send, recv, device):
        return pltpu.make_async_remote_copy(src, dst, send, recv, device_id=device, device_id_type=MESH)

    def await_bytes(ref, sem):
        pltpu.make_async_copy(ref, ref, sem).wait()

    barrier = pltpu.get_barrier_semaphore()
    others = [above, below, spouse] + [near(n % 4, n // 4) for n in range(1, 16)]
    others += [{"dp": (1 - yh) * 4 + lax.rem(xx + k, 4)} for k in range(4)]
    for device in others:
        pl.semaphore_signal(barrier, inc=1, device_id=device, device_id_type=MESH)

    half = pl.ds(pl.multiple_of(yh * 2048, 2048), 2048)
    other_half = pl.ds(pl.multiple_of((1 - yh) * 2048, 2048), 2048)
    local = [
        pltpu.make_async_copy(gu.at[0, :, :, half], w.at[pl.ds(0, 2)], loc.at[0]),
        pltpu.make_async_copy(down.at[0], wd, loc.at[1]),
    ]
    for c in local:
        c.start()

    lane = iota((TOK, 128), 1)
    place_f = place[...].astype(F32)
    hi = weight[...].astype(BF).astype(F32)
    lo = (weight[...] - hi).astype(BF).astype(F32)
    slots = []
    has = jnp.zeros((TOK, 128), F32)
    facts = jnp.zeros((TOK, 128), F32)
    for k in range(8):
        hit = ids[:, k : k + 1] == iota((TOK, NE), 1)
        slot = jnp.sum(jnp.where(hit, place_f, 0.0), axis=1, keepdims=True)
        slots.append(slot)
        has = has + jnp.where(slot == lane.astype(F32), 1.0, 0.0)
        facts = facts + jnp.where(lane == k, slot, 0.0)
        facts = facts + jnp.where(lane == 16 + k, hi[:, k : k + 1], 0.0) + jnp.where(lane == 24 + k, lo[:, k : k + 1], 0.0)
    before = flag(iota((TOK, TOK), 1) < iota((TOK, TOK), 0))
    count = dot(before, has.astype(BF))
    for k in range(8):
        pos = jnp.sum(jnp.where(slots[k] == lane.astype(F32), count, 0.0), axis=1, keepdims=True)
        facts = facts + jnp.where(lane == 8 + k, pos, 0.0)
    turned = dot(facts.astype(BF), flag(iota((TOK, TOK), 0) == iota((TOK, TOK), 1)), TN).astype(BF)
    ring[z, :TOK, :] = tokens[...]
    ring[z, TOK:, 0:128] = turned[0:16]
    ring[z, TOK:, 128:256] = turned[16:32]
    ring[z, TOK:, 256:384] = jnp.zeros((16, 128), BF)
    early = [
        remote(gu.at[0, 0, pl.ds(0, 48)], got_gu.at[0, 0, pl.ds(0, 48)], snd.at[9], rcv.at[3], spouse),
        remote(down.at[0, pl.ds(0, 384)], got_down.at[0, pl.ds(0, 384)], snd.at[10], rcv.at[4], spouse),
    ]
    ring[z, TOK:, 384:512] = dot(flag(iota((16, TOK), 0) == 0), has.astype(BF)).astype(BF)

    pl.semaphore_wait(barrier, len(others))

    def pass_up(block, s):
        remote(ring.at[block], ring.at[block], snd.at[0], ru.at[s], above).start()

    def pass_down(block, s):
        remote(ring.at[block], ring.at[block], snd.at[1], rd.at[s], below).start()

    pass_up(z, 0)
    pass_down(z, 0)

    trade = remote(gu.at[0, :, :, other_half], w.at[pl.ds(2, 2)], snd.at[3], rcv.at[1], across)
    trade.start()

    def by_slot(facts, values):
        return [
            jnp.sum(jnp.where(facts == (z * 4 + j).astype(F32), values, 0.0), axis=0, keepdims=True) for j in range(4)
        ]

    def picked(block):
        facts = ring[block, TOK:, 0:128].astype(F32)
        slot = facts[0:8]
        places = [v - 1.0 for v in by_slot(slot, facts[8:16] + 1.0)]
        return slot, over_rows(places) == row_number()

    def choose(block, n):
        rows = dot(flag(picked(block)[1]), ring[block, :TOK, :])
        more = rows[64:]
        third = flag((iota((16, 16), 0) % EXT == 3) & (iota((16, 16), 1) == 0))
        tally = dot(third, ring[block, TOK:, 384:512])
        more = tall(jnp.concatenate([more[:, :128] + tally, more[:, 128:]], axis=1)).astype(BF)
        pick[:, n, :, :FEAT] = rows[:64].astype(BF).reshape(4, MAIN, FEAT)
        pick[:, n, :, FEAT:] = dot(shuffle4(), more).astype(BF).reshape(4, MAIN, 128)

    def deal(n, blocks):
        src, dst = pl.ds(n, blocks), pl.ds(xx * NE + col * NZ + n, blocks)
        for m in range(1, 16):
            i, k = m % 4, m // 4
            j = lax.rem(col + i, 4)
            remote(pick.at[j, src], x_all.at[dst], snd.at[2], rcv.at[0], near(i, k)).start()
        pltpu.make_async_copy(pick.at[col, src], x_all.at[dst], loc.at[2]).start()

    choose(z, 0)
    deal(0, 1)

    def around(s, carry):
        low, high = lax.rem(z + 15 - s, NZ), lax.rem(z + 1 + s, NZ)
        await_bytes(ring.at[low], ru.at[s])
        pass_up(low, s + 1)
        await_bytes(ring.at[high], rd.at[s])

        @pl.when(s < 6)
        def _():
            pass_down(high, s + 1)

        choose(low, 2 * s + 1)
        choose(high, 2 * s + 2)
        deal(2 * s + 1, 2)
        return carry

    lax.fori_loop(0, 7, around, 0)
    far = lax.rem(z + 8, NZ)
    await_bytes(ring.at[far], ru.at[7])
    choose(far, 15)
    deal(15, 1)

    for c in local:
        c.wait()
    trade.wait_recv()
    await_bytes(x_all.at[pl.ds(0, 15 * NZ)], rcv.at[0])
    await_bytes(x_all.at[pl.ds(0, NZ)], loc.at[2])
    for c in early:
        c.start()

    q8 = shuffle8()

    def project(t, rows_of):
        total = jnp.zeros((4 * UNITS, TILE), F32)
        for x in range(4):
            part = w[:, :, x * FEAT : x * FEAT + FEAT].reshape(4 * UNITS, FEAT)
            total = total + dot(part, rows_of(x), NT)
        p_own[t] = total[: 2 * UNITS]
        p_send[t] = total[2 * UNITS :]
        remote(p_send.at[t], p_in.at[t], snd.at[4], pr.at[t], across).start()

    def further_rows(x):
        for b in range(8):
            packed = x_all[x * NE + 8 * b : x * NE + 8 * b + 8, :, FEAT:].reshape(128, 128)
            ext[32 * b : 32 * b + 32, :] = broad(dot(q8, packed, TN).astype(BF))
        if x == 0:
            totals[...] = dot(flag(iota((8, NE * EXT), 1) % EXT == 3), ext[:, :128])
        return ext[...]

    def project_tile(t, carry):
        project(t, lambda x: x_all[pl.ds(x * NE + t * 16, 16), :, :FEAT].reshape(TILE, FEAT))
        return carry

    project(4, further_rows)
    lax.fori_loop(0, 4, project_tile, 0)

    def activate(n, carry):
        t = lax.rem(n + 4, TILES)
        await_bytes(p_in.at[t], pr.at[t])
        both = p_own[t] + p_in[t]
        gate, up = both[:UNITS], both[UNITS:]
        hid[t, dp] = (gate / (1.0 + jnp.exp(-gate)) * up).astype(BF)
        for i in range(1, 8):
            remote(hid.at[t, dp], hid.at[t, dp], snd.at[5], hr.at[t], peer(i)).start()
        return carry

    lax.fori_loop(0, TILES, activate, 0)

    def produce(t):
        await_bytes(hid.at[t, pl.ds(0, 7)], hr.at[t])
        return dot(hid[t].reshape(8 * UNITS, TILE), wd[...], TN).astype(BF)

    ext[...] = produce(4)

    def finish(j):
        rows = pl.ds(j * 16, 16)
        y_send[rows, :, :FEAT] = produce(j).reshape(16, MAIN, FEAT)
        for g in range(2):
            more = tall(ext[pl.ds(pl.multiple_of(j * 64 + g * 32, 32), 32), :])
            y_send[pl.ds(j * 16 + g * 8, 8), :, FEAT:] = dot(q8, more).astype(BF).reshape(8, MAIN, 128)
        return y_send.at[rows]

    def give_back(i, carry):
        ref = finish(lax.rem(col + i, 4))
        remote(ref, y_in.at[col], snd.at[6], rcv.at[2], near(i)).start()
        return carry

    lax.fori_loop(1, 4, give_back, 0)
    mine = pltpu.make_async_copy(finish(col), y_in.at[col], loc.at[3])
    mine.start()
    await_bytes(y_in.at[pl.ds(0, 3)], rcv.at[2])
    mine.wait()

    def combine(block, n):
        slot, at = picked(block)
        terms = ring[block, TOK:, 128:256].astype(F32)
        more = broad(dot(shuffle4(), y_in[:, n, :, FEAT:].reshape(64, 128), TN).astype(BF))
        rows = jnp.concatenate([y_in[:, n, :, :FEAT].reshape(64, FEAT), more], axis=0)
        share = jnp.zeros((TOK, FEAT), F32)
        for part in range(2):
            mix = jnp.where(at, over_rows(by_slot(slot, terms[8 * part : 8 * part + 8])), 0.0)
            share = share + dot(mix.astype(BF), rows, TN)
        return share

    def hand_up(s, total):
        up_out[s] = total.astype(BF)
        remote(up_out.at[s], up_in.at[s], snd.at[7], su.at[s], above).start()

    def hand_down(s, total):
        dn_out[s] = total.astype(BF)
        remote(dn_out.at[s], dn_in.at[s], snd.at[8], sd.at[s], below).start()

    hand_up(0, combine(far, 15))
    hand_down(0, combine(lax.rem(z + 9, NZ), 13))

    def home(s, carry):
        share = combine(lax.rem(z + 8 - s, NZ), 16 - 2 * s)
        await_bytes(up_in.at[s - 1], su.at[s - 1])
        hand_up(s, share + up_in[s - 1].astype(F32))
        share = combine(lax.rem(z + 9 + s, NZ), 13 - 2 * s)
        await_bytes(dn_in.at[s - 1], sd.at[s - 1])
        hand_down(s, share + dn_in[s - 1].astype(F32))
        return carry

    lax.fori_loop(1, 7, home, 0)
    share = combine(lax.rem(z + 1, NZ), 2)
    await_bytes(up_in.at[6], su.at[6])
    hand_up(7, share + up_in[6].astype(F32))
    share = combine(z, 0)
    await_bytes(dn_in.at[6], sd.at[6])
    share = share + dn_in[6].astype(F32)
    await_bytes(up_in.at[7], su.at[7])
    out[...] = (share + up_in[7].astype(F32)).astype(BF)

    await_bytes(ring.at[pl.ds(0, 8)], snd.at[0])
    await_bytes(ring.at[pl.ds(0, 7)], snd.at[1])
    await_bytes(x_all.at[pl.ds(0, 15 * NZ)], snd.at[2])
    trade.wait_send()
    await_bytes(p_in, snd.at[4])
    await_bytes(hid.at[:, pl.ds(0, 7)], snd.at[5])
    await_bytes(y_in.at[pl.ds(0, 3)], snd.at[6])
    await_bytes(up_out, snd.at[7])
    await_bytes(dn_out, snd.at[8])
    for c in early:
        c.wait()


def exchange_kernel(pairs, gu, down, old_gu, old_down, got_gu, got_down, snd, rcv):
    me = lax.axis_index("expert")
    spouse = {"expert": lax.rem(me + NE // 2, NE)}

    own = lax.rem(me, NE // 2)
    taking_part = own == pairs[0]
    for pair in pairs[1:]:
        taking_part = taking_part | (own == pair)

    @pl.when(taking_part)
    def _():
        barrier = pltpu.get_barrier_semaphore()
        pl.semaphore_signal(barrier, inc=1, device_id=spouse, device_id_type=MESH)
        pl.semaphore_wait(barrier, 1)
        parts = [(gu, got_gu, (0, 1)), (gu, got_gu, (0, 0, pl.ds(48, 48))), (down, got_down, (0, pl.ds(384, 384)))]
        copies = [
            pltpu.make_async_remote_copy(
                src.at[at], dst.at[at], snd.at[n], rcv.at[n], device_id=spouse, device_id_type=MESH
            )
            for n, (src, dst, at) in enumerate(parts)
        ]
        for c in copies:
            c.start()
        for c in copies:
            c.wait()


def exchange(pairs, number, gu, down, old_gu, old_down):
    hbm = pl.BlockSpec(memory_space=pl.ANY)
    return tuple(
        pl.pallas_call(
            functools.partial(exchange_kernel, pairs),
            out_shape=[jax.ShapeDtypeStruct(old_gu.shape, BF), jax.ShapeDtypeStruct(old_down.shape, BF)],
            in_specs=[hbm] * 4,
            out_specs=[hbm] * 2,
            input_output_aliases={2: 0, 3: 1},
            scratch_shapes=[pltpu.SemaphoreType.DMA((3,)), pltpu.SemaphoreType.DMA((3,))],
            compiler_params=pltpu.CompilerParams(collective_id=number, has_side_effects=True),
            name="exchange",
        )(gu, down, old_gu, old_down)
    )


def body(tokens, expert_ids, route_weight, placement, swap_flag, gate_up, down_weight):
    vmem = pl.BlockSpec(memory_space=pltpu.VMEM)
    hbm = pl.BlockSpec(memory_space=pl.ANY)
    moe_out, totals, *got = pl.pallas_call(
        kernel,
        out_shape=[
            jax.ShapeDtypeStruct((TOK, FEAT), BF),
            jax.ShapeDtypeStruct((8, 128), F32),
            jax.ShapeDtypeStruct(gate_up.shape, BF),
            jax.ShapeDtypeStruct(down_weight.shape, BF),
        ],
        in_specs=[vmem, vmem, vmem, vmem, hbm, hbm],
        out_specs=[vmem, vmem, hbm, hbm],
        scratch_shapes=[
            pltpu.VMEM((NZ, TOK + 16, FEAT), BF),
            pltpu.VMEM((4, NZ, MAIN, WIDE), BF),
            pltpu.VMEM((4 * NE, MAIN, WIDE), BF),
            pltpu.VMEM((4, UNITS, 4 * FEAT), BF),
            pltpu.VMEM((8 * UNITS, FEAT), BF),
            pltpu.VMEM((TILES, 2 * UNITS, TILE), F32),
            pltpu.VMEM((TILES, 2 * UNITS, TILE), F32),
            pltpu.VMEM((TILES, 2 * UNITS, TILE), F32),
            pltpu.VMEM((TILES, 8, UNITS, TILE), BF),
            pltpu.VMEM((NE * EXT, FEAT), BF),
            pltpu.VMEM((NE, MAIN, WIDE), BF),
            pltpu.VMEM((4, NZ, MAIN, WIDE), BF),
            pltpu.VMEM((8, TOK, FEAT), BF),
            pltpu.VMEM((8, TOK, FEAT), BF),
            pltpu.VMEM((7, TOK, FEAT), BF),
            pltpu.VMEM((7, TOK, FEAT), BF),
            pltpu.SemaphoreType.DMA((11,)),
            pltpu.SemaphoreType.DMA((5,)),
            pltpu.SemaphoreType.DMA((8,)),
            pltpu.SemaphoreType.DMA((7,)),
            pltpu.SemaphoreType.DMA((TILES,)),
            pltpu.SemaphoreType.DMA((TILES,)),
            pltpu.SemaphoreType.DMA((8,)),
            pltpu.SemaphoreType.DMA((7,)),
            pltpu.SemaphoreType.DMA((4,)),
        ],
        compiler_params=pltpu.CompilerParams(
            collective_id=0, has_side_effects=True, vmem_limit_bytes=48 << 20
        ),
        cost_estimate=pl.CostEstimate(flops=5_000_000_000, bytes_accessed=10_000_000, transcendentals=200_000),
        name="experts",
    )(tokens, expert_ids, route_weight, placement.reshape(1, NE), gate_up, down_weight)
    chosen = jnp.sum(swap_flag.reshape(8, 4) * jnp.array([1, 2, 4, 8], jnp.int32), axis=1)
    for group in range(8):
        sets = [lambda gu, down, got_gu, got_down: (got_gu, got_down)]
        for number in range(1, 16):
            pairs = tuple(group * 4 + n for n in range(4) if number >> n & 1)
            sets.append(functools.partial(exchange, pairs, group * 15 + number))
        got = lax.switch(chosen[group], sets, gate_up, down_weight, *got)
    got_gu, got_down = got
    flags = jnp.concatenate([swap_flag, swap_flag]) == 1
    load = totals[0, :NE]
    column_load = jnp.where(flags, jnp.roll(load, NE // 2), load) / jnp.float32(TOK * 8)
    mine = jnp.arange(NE // 2, dtype=jnp.int32) == lax.axis_index("expert") % (NE // 2)
    swapped = jnp.sum(jnp.where(mine, swap_flag, 0)) == 1
    return (
        moe_out,
        column_load,
        jnp.where(swapped, got_gu, gate_up),
        jnp.where(swapped, got_down, down_weight),
    )


def solution(mesh):
    return jax.shard_map(
        body,
        mesh=mesh,
        in_specs=(
            P("expert", "dp"),
            P("expert", None),
            P("expert", None),
            P(),
            P(),
            P("expert", None, "dp", None),
            P("expert", None, "dp"),
        ),
        out_specs=(P("expert", "dp"), P(), P("expert", None, "dp", None), P("expert", None, "dp")),
        check_vma=False,
    )
```

```python
import functools

import jax
import jax.numpy as jnp
from jax import lax
from jax.experimental import pallas as pl
from jax.experimental.pallas import tpu as pltpu
from jax.sharding import PartitionSpec as P

MESH = pl.DeviceIdType.MESH
BF = jnp.bfloat16
F32 = jnp.float32
NN = (((1,), (0,)), ((), ()))
NT = (((1,), (1,)), ((), ()))
TN = (((0,), (0,)), ((), ()))

NE = 64
NZ = 16
TOK = 128
FEAT = 512
MAIN, EXT = 16, 4
WIDE = FEAT + 128
UNITS = 96
TILE = 256
TILES = 5


def iota(shape, axis):
    return lax.broadcasted_iota(jnp.int32, shape, axis)


def flag(cond):
    return jnp.where(cond, 1.0, 0.0).astype(BF)


def dot(a, b, dims=NN):
    return lax.dot_general(a, b, dims, preferred_element_type=F32)


def shuffle8():
    row, col = iota((128, 128), 0), iota((128, 128), 1)
    return flag(((row % 16) // 4) * 32 + (row // 16) * 4 + row % 4 == col)


def shuffle4():
    row, col = iota((64, 64), 0), iota((64, 64), 1)
    return flag(((row % 16) // 4) * 16 + (row // 16) * 4 + row % 4 == col)


def tall(rows):
    return jnp.concatenate([rows[:, 128 * c : 128 * c + 128] for c in range(4)], axis=0)


def broad(rows):
    n = rows.shape[0] // 4
    return jnp.concatenate([rows[n * c : n * c + n] for c in range(4)], axis=1)


def over_rows(values):
    row = iota((16, TOK), 0) // EXT
    last = sum(jnp.where(row == j, values[j], 0.0) for j in range(4))
    return jnp.concatenate([jnp.broadcast_to(v, (MAIN, TOK)) for v in values] + [last], axis=0)


def row_number():
    row = iota((80, TOK), 0)
    return jnp.where(row < 64, row % MAIN, MAIN + row % EXT).astype(F32)


def kernel(
    tokens, ids, weight, place, gu, down,
    out, totals, got_gu, got_down,
    ring, pick, x_all, w, wd, p_send, p_own, p_in, hid, ext, y_send, y_in, up_out, up_in, dn_out, dn_in,
    snd, rcv, ru, rd, pr, hr, su, sd, loc,
):
    dp, me = lax.axis_index("dp"), lax.axis_index("expert")
    z, col = me // 4, lax.rem(me, 4)
    above, below = {"expert": lax.rem(me + 4, NE)}, {"expert": lax.rem(me + NE - 4, NE)}
    spouse = {"expert": lax.rem(me + 32, NE)}

    yh, xx = dp // 4, lax.rem(dp, 4)
    across = {"dp": lax.rem(dp + 4, 8)}

    def near(i, k=0):
        return {"dp": yh * 4 + lax.rem(xx + k, 4), "expert": z * 4 + lax.rem(col + i, 4)}

    def peer(i):
        return {"dp": lax.rem(dp + i, 8)}

    def remote(src, dst, send, recv, device):
        return pltpu.make_async_remote_copy(src, dst, send, recv, device_id=device, device_id_type=MESH)

    def await_bytes(ref, sem):
        pltpu.make_async_copy(ref, ref, sem).wait()

    barrier = pltpu.get_barrier_semaphore()
    others = [above, below, spouse] + [near(n % 4, n // 4) for n in range(1, 16)]
    others += [{"dp": (1 - yh) * 4 + lax.rem(xx + k, 4)} for k in range(4)]
    for device in others:
        pl.semaphore_signal(barrier, inc=1, device_id=device, device_id_type=MESH)

    half = pl.ds(pl.multiple_of(yh * 2048, 2048), 2048)
    other_half = pl.ds(pl.multiple_of((1 - yh) * 2048, 2048), 2048)
    local = [
        pltpu.make_async_copy(gu.at[0, :, :, half], w.at[pl.ds(0, 2)], loc.at[0]),
        pltpu.make_async_copy(down.at[0], wd, loc.at[1]),
    ]
    for c in local:
        c.start()

    lane = iota((TOK, 128), 1)
    place_f = place[...].astype(F32)
    hi = weight[...].astype(BF).astype(F32)
    lo = (weight[...] - hi).astype(BF).astype(F32)
    slots = []
    has = jnp.zeros((TOK, 128), F32)
    facts = jnp.zeros((TOK, 128), F32)
    for k in range(8):
        hit = ids[:, k : k + 1] == iota((TOK, NE), 1)
        slot = jnp.sum(jnp.where(hit, place_f, 0.0), axis=1, keepdims=True)
        slots.append(slot)
        has = has + jnp.where(slot == lane.astype(F32), 1.0, 0.0)
        facts = facts + jnp.where(lane == k, slot, 0.0)
        facts = facts + jnp.where(lane == 16 + k, hi[:, k : k + 1], 0.0) + jnp.where(lane == 24 + k, lo[:, k : k + 1], 0.0)
    before = flag(iota((TOK, TOK), 1) < iota((TOK, TOK), 0))
    count = dot(before, has.astype(BF))
    for k in range(8):
        pos = jnp.sum(jnp.where(slots[k] == lane.astype(F32), count, 0.0), axis=1, keepdims=True)
        facts = facts + jnp.where(lane == 8 + k, pos, 0.0)
    turned = dot(facts.astype(BF), flag(iota((TOK, TOK), 0) == iota((TOK, TOK), 1)), TN).astype(BF)
    ring[z, :TOK, :] = tokens[...]
    ring[z, TOK:, 0:128] = turned[0:16]
    ring[z, TOK:, 128:256] = turned[16:32]
    ring[z, TOK:, 256:384] = jnp.zeros((16, 128), BF)
    early = [
        remote(gu.at[0, 0, pl.ds(0, 48)], got_gu.at[0, 0, pl.ds(0, 48)], snd.at[9], rcv.at[3], spouse),
        remote(down.at[0, pl.ds(0, 384)], got_down.at[0, pl.ds(0, 384)], snd.at[10], rcv.at[4], spouse),
    ]
    ring[z, TOK:, 384:512] = dot(flag(iota((16, TOK), 0) == 0), has.astype(BF)).astype(BF)

    pl.semaphore_wait(barrier, len(others))

    def pass_up(block, s):
        remote(ring.at[block], ring.at[block], snd.at[0], ru.at[s], above).start()

    def pass_down(block, s):
        remote(ring.at[block], ring.at[block], snd.at[1], rd.at[s], below).start()

    pass_up(z, 0)
    pass_down(z, 0)

    trade = remote(gu.at[0, :, :, other_half], w.at[pl.ds(2, 2)], snd.at[3], rcv.at[1], across)
    trade.start()

    def by_slot(facts, values):
        return [
            jnp.sum(jnp.where(facts == (z * 4 + j).astype(F32), values, 0.0), axis=0, keepdims=True) for j in range(4)
        ]

    def picked(block):
        facts = ring[block, TOK:, 0:128].astype(F32)
        slot = facts[0:8]
        places = [v - 1.0 for v in by_slot(slot, facts[8:16] + 1.0)]
        return slot, over_rows(places) == row_number()

    def choose(block, n):
        rows = dot(flag(picked(block)[1]), ring[block, :TOK, :])
        more = rows[64:]
        third = flag((iota((16, 16), 0) % EXT == 3) & (iota((16, 16), 1) == 0))
        tally = dot(third, ring[block, TOK:, 384:512])
        more = tall(jnp.concatenate([more[:, :128] + tally, more[:, 128:]], axis=1)).astype(BF)
        pick[:, n, :, :FEAT] = rows[:64].astype(BF).reshape(4, MAIN, FEAT)
        pick[:, n, :, FEAT:] = dot(shuffle4(), more).astype(BF).reshape(4, MAIN, 128)

    def deal(n, blocks):
        src, dst = pl.ds(n, blocks), pl.ds(xx * NE + col * NZ + n, blocks)
        for m in range(1, 16):
            i, k = m % 4, m // 4
            j = lax.rem(col + i, 4)
            remote(pick.at[j, src], x_all.at[dst], snd.at[2], rcv.at[0], near(i, k)).start()
        pltpu.make_async_copy(pick.at[col, src], x_all.at[dst], loc.at[2]).start()

    choose(z, 0)
    deal(0, 1)

    def around(s, carry):
        low, high = lax.rem(z + 15 - s, NZ), lax.rem(z + 1 + s, NZ)
        await_bytes(ring.at[low], ru.at[s])
        pass_up(low, s + 1)
        await_bytes(ring.at[high], rd.at[s])

        @pl.when(s < 6)
        def _():
            pass_down(high, s + 1)

        choose(low, 2 * s + 1)
        choose(high, 2 * s + 2)
        deal(2 * s + 1, 2)
        return carry

    lax.fori_loop(0, 7, around, 0)
    far = lax.rem(z + 8, NZ)
    await_bytes(ring.at[far], ru.at[7])
    choose(far, 15)
    deal(15, 1)

    for c in local:
        c.wait()
    trade.wait_recv()
    await_bytes(x_all.at[pl.ds(0, 15 * NZ)], rcv.at[0])
    await_bytes(x_all.at[pl.ds(0, NZ)], loc.at[2])
    for c in early:
        c.start()

    q8 = shuffle8()

    def project(t, rows_of):
        total = jnp.zeros((4 * UNITS, TILE), F32)
        for x in range(4):
            part = w[:, :, x * FEAT : x * FEAT + FEAT].reshape(4 * UNITS, FEAT)
            total = total + dot(part, rows_of(x), NT)
        p_own[t] = total[: 2 * UNITS]
        p_send[t] = total[2 * UNITS :]
        remote(p_send.at[t], p_in.at[t], snd.at[4], pr.at[t], across).start()

    def further_rows(x):
        for b in range(8):
            packed = x_all[x * NE + 8 * b : x * NE + 8 * b + 8, :, FEAT:].reshape(128, 128)
            ext[32 * b : 32 * b + 32, :] = broad(dot(q8, packed, TN).astype(BF))
        if x == 0:
            totals[...] = dot(flag(iota((8, NE * EXT), 1) % EXT == 3), ext[:, :128])
        return ext[...]

    def project_tile(t, carry):
        project(t, lambda x: x_all[pl.ds(x * NE + t * 16, 16), :, :FEAT].reshape(TILE, FEAT))
        return carry

    project(4, further_rows)
    lax.fori_loop(0, 4, project_tile, 0)

    def activate(n, carry):
        t = lax.rem(n + 4, TILES)
        await_bytes(p_in.at[t], pr.at[t])
        both = p_own[t] + p_in[t]
        gate, up = both[:UNITS], both[UNITS:]
        hid[t, dp] = (gate / (1.0 + jnp.exp(-gate)) * up).astype(BF)
        for i in range(1, 8):
            remote(hid.at[t, dp], hid.at[t, dp], snd.at[5], hr.at[t], peer(i)).start()
        return carry

    lax.fori_loop(0, TILES, activate, 0)

    def produce(t):
        await_bytes(hid.at[t, pl.ds(0, 7)], hr.at[t])
        return dot(hid[t].reshape(8 * UNITS, TILE), wd[...], TN).astype(BF)

    ext[...] = produce(4)

    def finish(j):
        rows = pl.ds(j * 16, 16)
        y_send[rows, :, :FEAT] = produce(j).reshape(16, MAIN, FEAT)
        for g in range(2):
            more = tall(ext[pl.ds(pl.multiple_of(j * 64 + g * 32, 32), 32), :])
            y_send[pl.ds(j * 16 + g * 8, 8), :, FEAT:] = dot(q8, more).astype(BF).reshape(8, MAIN, 128)
        return y_send.at[rows]

    def give_back(i, carry):
        ref = finish(lax.rem(col + i, 4))
        remote(ref, y_in.at[col], snd.at[6], rcv.at[2], near(i)).start()
        return carry

    lax.fori_loop(1, 4, give_back, 0)
    mine = pltpu.make_async_copy(finish(col), y_in.at[col], loc.at[3])
    mine.start()
    await_bytes(y_in.at[pl.ds(0, 3)], rcv.at[2])
    mine.wait()

    def combine(block, n):
        slot, at = picked(block)
        terms = ring[block, TOK:, 128:256].astype(F32)
        more = broad(dot(shuffle4(), y_in[:, n, :, FEAT:].reshape(64, 128), TN).astype(BF))
        rows = jnp.concatenate([y_in[:, n, :, :FEAT].reshape(64, FEAT), more], axis=0)
        share = jnp.zeros((TOK, FEAT), F32)
        for part in range(2):
            mix = jnp.where(at, over_rows(by_slot(slot, terms[8 * part : 8 * part + 8])), 0.0)
            share = share + dot(mix.astype(BF), rows, TN)
        return share

    def hand_up(s, total):
        up_out[s] = total.astype(BF)
        remote(up_out.at[s], up_in.at[s], snd.at[7], su.at[s], above).start()

    def hand_down(s, total):
        dn_out[s] = total.astype(BF)
        remote(dn_out.at[s], dn_in.at[s], snd.at[8], sd.at[s], below).start()

    hand_up(0, combine(far, 15))
    hand_down(0, combine(lax.rem(z + 9, NZ), 13))

    def home(s, carry):
        share = combine(lax.rem(z + 8 - s, NZ), 16 - 2 * s)
        await_bytes(up_in.at[s - 1], su.at[s - 1])
        hand_up(s, share + up_in[s - 1].astype(F32))
        share = combine(lax.rem(z + 9 + s, NZ), 13 - 2 * s)
        await_bytes(dn_in.at[s - 1], sd.at[s - 1])
        hand_down(s, share + dn_in[s - 1].astype(F32))
        return carry

    lax.fori_loop(1, 7, home, 0)
    share = combine(lax.rem(z + 1, NZ), 2)
    await_bytes(up_in.at[6], su.at[6])
    hand_up(7, share + up_in[6].astype(F32))
    share = combine(z, 0)
    await_bytes(dn_in.at[6], sd.at[6])
    share = share + dn_in[6].astype(F32)
    await_bytes(up_in.at[7], su.at[7])
    out[...] = (share + up_in[7].astype(F32)).astype(BF)

    await_bytes(ring.at[pl.ds(0, 8)], snd.at[0])
    await_bytes(ring.at[pl.ds(0, 7)], snd.at[1])
    await_bytes(x_all.at[pl.ds(0, 15 * NZ)], snd.at[2])
    trade.wait_send()
    await_bytes(p_in, snd.at[4])
    await_bytes(hid.at[:, pl.ds(0, 7)], snd.at[5])
    await_bytes(y_in.at[pl.ds(0, 3)], snd.at[6])
    await_bytes(up_out, snd.at[7])
    await_bytes(dn_out, snd.at[8])
    for c in early:
        c.wait()


def exchange_kernel(pair, gu, down, old_gu, old_down, got_gu, got_down, snd, rcv):
    me = lax.axis_index("expert")
    spouse = {"expert": lax.rem(me + NE // 2, NE)}

    @pl.when(lax.rem(me, NE // 2) == pair)
    def _():
        barrier = pltpu.get_barrier_semaphore()
        pl.semaphore_signal(barrier, inc=1, device_id=spouse, device_id_type=MESH)
        pl.semaphore_wait(barrier, 1)
        parts = [(gu, got_gu, (0, 1)), (gu, got_gu, (0, 0, pl.ds(48, 48))), (down, got_down, (0, pl.ds(384, 384)))]
        copies = [
            pltpu.make_async_remote_copy(
                src.at[at], dst.at[at], snd.at[n], rcv.at[n], device_id=spouse, device_id_type=MESH
            )
            for n, (src, dst, at) in enumerate(parts)
        ]
        for c in copies:
            c.start()
        for c in copies:
            c.wait()


def exchange(pair, gu, down, old_gu, old_down):
    hbm = pl.BlockSpec(memory_space=pl.ANY)
    return tuple(
        pl.pallas_call(
            functools.partial(exchange_kernel, pair),
            out_shape=[jax.ShapeDtypeStruct(old_gu.shape, BF), jax.ShapeDtypeStruct(old_down.shape, BF)],
            in_specs=[hbm] * 4,
            out_specs=[hbm] * 2,
            input_output_aliases={2: 0, 3: 1},
            scratch_shapes=[pltpu.SemaphoreType.DMA((3,)), pltpu.SemaphoreType.DMA((3,))],
            compiler_params=pltpu.CompilerParams(collective_id=1 + pair, has_side_effects=True),
            name="exchange",
        )(gu, down, old_gu, old_down)
    )


def body(tokens, expert_ids, route_weight, placement, swap_flag, gate_up, down_weight):
    vmem = pl.BlockSpec(memory_space=pltpu.VMEM)
    hbm = pl.BlockSpec(memory_space=pl.ANY)
    moe_out, totals, *got = pl.pallas_call(
        kernel,
        out_shape=[
            jax.ShapeDtypeStruct((TOK, FEAT), BF),
            jax.ShapeDtypeStruct((8, 128), F32),
            jax.ShapeDtypeStruct(gate_up.shape, BF),
            jax.ShapeDtypeStruct(down_weight.shape, BF),
        ],
        in_specs=[vmem, vmem, vmem, vmem, hbm, hbm],
        out_specs=[vmem, vmem, hbm, hbm],
        scratch_shapes=[
            pltpu.VMEM((NZ, TOK + 16, FEAT), BF),
            pltpu.VMEM((4, NZ, MAIN, WIDE), BF),
            pltpu.VMEM((4 * NE, MAIN, WIDE), BF),
            pltpu.VMEM((4, UNITS, 4 * FEAT), BF),
            pltpu.VMEM((8 * UNITS, FEAT), BF),
            pltpu.VMEM((TILES, 2 * UNITS, TILE), F32),
            pltpu.VMEM((TILES, 2 * UNITS, TILE), F32),
            pltpu.VMEM((TILES, 2 * UNITS, TILE), F32),
            pltpu.VMEM((TILES, 8, UNITS, TILE), BF),
            pltpu.VMEM((NE * EXT, FEAT), BF),
            pltpu.VMEM((NE, MAIN, WIDE), BF),
            pltpu.VMEM((4, NZ, MAIN, WIDE), BF),
            pltpu.VMEM((8, TOK, FEAT), BF),
            pltpu.VMEM((8, TOK, FEAT), BF),
            pltpu.VMEM((7, TOK, FEAT), BF),
            pltpu.VMEM((7, TOK, FEAT), BF),
            pltpu.SemaphoreType.DMA((11,)),
            pltpu.SemaphoreType.DMA((5,)),
            pltpu.SemaphoreType.DMA((8,)),
            pltpu.SemaphoreType.DMA((7,)),
            pltpu.SemaphoreType.DMA((TILES,)),
            pltpu.SemaphoreType.DMA((TILES,)),
            pltpu.SemaphoreType.DMA((8,)),
            pltpu.SemaphoreType.DMA((7,)),
            pltpu.SemaphoreType.DMA((4,)),
        ],
        compiler_params=pltpu.CompilerParams(
            collective_id=0, has_side_effects=True, vmem_limit_bytes=48 << 20
        ),
        cost_estimate=pl.CostEstimate(flops=5_000_000_000, bytes_accessed=10_000_000, transcendentals=200_000),
        name="experts",
    )(tokens, expert_ids, route_weight, placement.reshape(1, NE), gate_up, down_weight)
    word = jnp.sum(swap_flag[: NE // 2] << jnp.arange(NE // 2, dtype=jnp.int32))
    word = lax.optimization_barrier(word)
    for pair in range(NE // 2):
        got = lax.cond(
            (word >> pair) & 1 == 1,
            functools.partial(exchange, pair),
            lambda gu, down, got_gu, got_down: (got_gu, got_down),
            gate_up, down_weight, *got,
        )
    got_gu, got_down = got
    flags = jnp.concatenate([swap_flag, swap_flag]) == 1
    load = totals[0, :NE]
    column_load = jnp.where(flags, jnp.roll(load, NE // 2), load) / jnp.float32(TOK * 8)
    mine = jnp.arange(NE // 2, dtype=jnp.int32) == lax.axis_index("expert") % (NE // 2)
    swapped = jnp.sum(jnp.where(mine, swap_flag, 0)) == 1
    return (
        moe_out,
        column_load,
        jnp.where(swapped, got_gu, gate_up),
        jnp.where(swapped, got_down, down_weight),
    )


def solution(mesh):
    return jax.shard_map(
        body,
        mesh=mesh,
        in_specs=(
            P("expert", "dp"),
            P("expert", None),
            P("expert", None),
            P(),
            P(),
            P("expert", None, "dp", None),
            P("expert", None, "dp"),
        ),
        out_specs=(P("expert", "dp"), P(), P("expert", None, "dp", None), P("expert", None, "dp")),
        check_vma=False,
    )
```

```python
import functools

import jax
import jax.numpy as jnp
from jax import lax
from jax.experimental import pallas as pl
from jax.experimental.pallas import tpu as pltpu
from jax.sharding import PartitionSpec as P

MESH = pl.DeviceIdType.MESH
BF = jnp.bfloat16
F32 = jnp.float32
NN = (((1,), (0,)), ((), ()))
NT = (((1,), (1,)), ((), ()))
TN = (((0,), (0,)), ((), ()))

NE = 64
NZ = 16
TOK = 128
FEAT = 512
MAIN, EXT = 16, 4
WIDE = FEAT + 128
UNITS = 96
TILE = 256
TILES = 5


def iota(shape, axis):
    return lax.broadcasted_iota(jnp.int32, shape, axis)


def flag(cond):
    return jnp.where(cond, 1.0, 0.0).astype(BF)


def dot(a, b, dims=NN):
    return lax.dot_general(a, b, dims, preferred_element_type=F32)


def shuffle8():
    row, col = iota((128, 128), 0), iota((128, 128), 1)
    return flag(((row % 16) // 4) * 32 + (row // 16) * 4 + row % 4 == col)


def shuffle4():
    row, col = iota((64, 64), 0), iota((64, 64), 1)
    return flag(((row % 16) // 4) * 16 + (row // 16) * 4 + row % 4 == col)


def tall(rows):
    return jnp.concatenate([rows[:, 128 * c : 128 * c + 128] for c in range(4)], axis=0)


def broad(rows):
    n = rows.shape[0] // 4
    return jnp.concatenate([rows[n * c : n * c + n] for c in range(4)], axis=1)


def over_rows(values):
    row = iota((16, TOK), 0) // EXT
    last = sum(jnp.where(row == j, values[j], 0.0) for j in range(4))
    return jnp.concatenate([jnp.broadcast_to(v, (MAIN, TOK)) for v in values] + [last], axis=0)


def row_number():
    row = iota((80, TOK), 0)
    return jnp.where(row < 64, row % MAIN, MAIN + row % EXT).astype(F32)


def kernel(
    tokens, ids, weight, place, gu, down,
    out, totals, got_gu, got_down,
    ring, pick, x_all, w, wd, p_send, p_own, p_in, hid, ext, y_send, y_in, up_out, up_in, dn_out, dn_in,
    snd, rcv, ru, rd, pr, hr, su, sd, loc,
):
    dp, me = lax.axis_index("dp"), lax.axis_index("expert")
    z, col = me // 4, lax.rem(me, 4)
    above, below = {"expert": lax.rem(me + 4, NE)}, {"expert": lax.rem(me + NE - 4, NE)}
    spouse = {"expert": lax.rem(me + 32, NE)}

    yh, xx = dp // 4, lax.rem(dp, 4)
    across = {"dp": lax.rem(dp + 4, 8)}

    def near(i, k=0):
        return {"dp": yh * 4 + lax.rem(xx + k, 4), "expert": z * 4 + lax.rem(col + i, 4)}

    def peer(i):
        return {"dp": lax.rem(dp + i, 8)}

    def remote(src, dst, send, recv, device):
        return pltpu.make_async_remote_copy(src, dst, send, recv, device_id=device, device_id_type=MESH)

    def await_bytes(ref, sem):
        pltpu.make_async_copy(ref, ref, sem).wait()

    barrier = pltpu.get_barrier_semaphore()
    others = [above, below, spouse] + [near(n % 4, n // 4) for n in range(1, 16)]
    others += [{"dp": (1 - yh) * 4 + lax.rem(xx + k, 4)} for k in range(4)]
    for device in others:
        pl.semaphore_signal(barrier, inc=1, device_id=device, device_id_type=MESH)

    half = pl.ds(pl.multiple_of(yh * 2048, 2048), 2048)
    other_half = pl.ds(pl.multiple_of((1 - yh) * 2048, 2048), 2048)
    local = [
        pltpu.make_async_copy(gu.at[0, :, :, half], w.at[pl.ds(0, 2)], loc.at[0]),
        pltpu.make_async_copy(down.at[0], wd, loc.at[1]),
    ]
    for c in local:
        c.start()

    lane = iota((TOK, 128), 1)
    place_f = place[...].astype(F32)
    hi = weight[...].astype(BF).astype(F32)
    lo = (weight[...] - hi).astype(BF).astype(F32)
    slots = []
    has = jnp.zeros((TOK, 128), F32)
    facts = jnp.zeros((TOK, 128), F32)
    for k in range(8):
        hit = ids[:, k : k + 1] == iota((TOK, NE), 1)
        slot = jnp.sum(jnp.where(hit, place_f, 0.0), axis=1, keepdims=True)
        slots.append(slot)
        has = has + jnp.where(slot == lane.astype(F32), 1.0, 0.0)
        facts = facts + jnp.where(lane == k, slot, 0.0)
        facts = facts + jnp.where(lane == 16 + k, hi[:, k : k + 1], 0.0) + jnp.where(lane == 24 + k, lo[:, k : k + 1], 0.0)
    before = flag(iota((TOK, TOK), 1) < iota((TOK, TOK), 0))
    count = dot(before, has.astype(BF))
    for k in range(8):
        pos = jnp.sum(jnp.where(slots[k] == lane.astype(F32), count, 0.0), axis=1, keepdims=True)
        facts = facts + jnp.where(lane == 8 + k, pos, 0.0)
    turned = dot(facts.astype(BF), flag(iota((TOK, TOK), 0) == iota((TOK, TOK), 1)), TN).astype(BF)
    ring[z, :TOK, :] = tokens[...]
    ring[z, TOK:, 0:128] = turned[0:16]
    ring[z, TOK:, 128:256] = turned[16:32]
    ring[z, TOK:, 256:384] = jnp.zeros((16, 128), BF)
    early = [
        remote(gu.at[0, 0, pl.ds(0, 48)], got_gu.at[0, 0, pl.ds(0, 48)], snd.at[9], rcv.at[3], spouse),
        remote(down.at[0, pl.ds(0, 384)], got_down.at[0, pl.ds(0, 384)], snd.at[10], rcv.at[4], spouse),
    ]
    ring[z, TOK:, 384:512] = dot(flag(iota((16, TOK), 0) == 0), has.astype(BF)).astype(BF)

    pl.semaphore_wait(barrier, len(others))

    def part_of(block, h):
        return ring.at[block, pl.ds(80 * h, 80 - 16 * h)]

    def pass_up(block, s, h):
        remote(part_of(block, h), part_of(block, h), snd.at[0], ru.at[2 * s + h], above).start()

    def pass_down(block, s, h):
        remote(part_of(block, h), part_of(block, h), snd.at[1], rd.at[2 * s + h], below).start()

    for h in range(2):
        pass_up(z, 0, h)
        pass_down(z, 0, h)
    trade = remote(gu.at[0, :, :, other_half], w.at[pl.ds(2, 2)], snd.at[3], rcv.at[1], across)
    trade.start()

    def by_slot(facts, values):
        return [
            jnp.sum(jnp.where(facts == (z * 4 + j).astype(F32), values, 0.0), axis=0, keepdims=True) for j in range(4)
        ]

    def picked(block):
        facts = ring[block, TOK:, 0:128].astype(F32)
        slot = facts[0:8]
        places = [v - 1.0 for v in by_slot(slot, facts[8:16] + 1.0)]
        return slot, over_rows(places) == row_number()

    def choose(block, n):
        rows = dot(flag(picked(block)[1]), ring[block, :TOK, :])
        more = rows[64:]
        third = flag((iota((16, 16), 0) % EXT == 3) & (iota((16, 16), 1) == 0))
        tally = dot(third, ring[block, TOK:, 384:512])
        more = tall(jnp.concatenate([more[:, :128] + tally, more[:, 128:]], axis=1)).astype(BF)
        pick[:, n, :, :FEAT] = rows[:64].astype(BF).reshape(4, MAIN, FEAT)
        pick[:, n, :, FEAT:] = dot(shuffle4(), more).astype(BF).reshape(4, MAIN, 128)

    def deal(n, blocks):
        src, dst = pl.ds(n, blocks), pl.ds(xx * NE + col * NZ + n, blocks)
        for m in range(1, 16):
            i, k = m % 4, m // 4
            j = lax.rem(col + i, 4)
            remote(pick.at[j, src], x_all.at[dst], snd.at[2], rcv.at[0], near(i, k)).start()
        pltpu.make_async_copy(pick.at[col, src], x_all.at[dst], loc.at[2]).start()

    choose(z, 0)
    deal(0, 1)

    def around(s, carry):
        low, high = lax.rem(z + 15 - s, NZ), lax.rem(z + 1 + s, NZ)
        for h in range(2):
            await_bytes(part_of(low, h), ru.at[2 * s + h])
            pass_up(low, s + 1, h)
            await_bytes(part_of(high, h), rd.at[2 * s + h])

            @pl.when(s < 6)
            def _(h=h):
                pass_down(high, s + 1, h)

        choose(low, 2 * s + 1)
        choose(high, 2 * s + 2)
        deal(2 * s + 1, 2)
        return carry

    lax.fori_loop(0, 7, around, 0)
    far = lax.rem(z + 8, NZ)
    for h in range(2):
        await_bytes(part_of(far, h), ru.at[14 + h])
    for c in early:
        c.start()
    choose(far, 15)
    deal(15, 1)

    for c in local:
        c.wait()
    trade.wait_recv()
    await_bytes(x_all.at[pl.ds(0, 15 * NZ)], rcv.at[0])
    await_bytes(x_all.at[pl.ds(0, NZ)], loc.at[2])

    q8 = shuffle8()

    def project(t, rows_of):
        total = jnp.zeros((4 * UNITS, TILE), F32)
        for x in range(4):
            part = w[:, :, x * FEAT : x * FEAT + FEAT].reshape(4 * UNITS, FEAT)
            total = total + dot(part, rows_of(x), NT)
        p_own[t] = total[: 2 * UNITS]
        p_send[t] = total[2 * UNITS :]
        remote(p_send.at[t], p_in.at[t], snd.at[4], pr.at[t], across).start()

    def further_rows(x):
        for b in range(8):
            packed = x_all[x * NE + 8 * b : x * NE + 8 * b + 8, :, FEAT:].reshape(128, 128)
            ext[32 * b : 32 * b + 32, :] = broad(dot(q8, packed, TN).astype(BF))
        if x == 0:
            totals[...] = dot(flag(iota((8, NE * EXT), 1) % EXT == 3), ext[:, :128])
        return ext[...]

    def project_tile(t, carry):
        project(t, lambda x: x_all[pl.ds(x * NE + t * 16, 16), :, :FEAT].reshape(TILE, FEAT))
        return carry

    project(4, further_rows)
    lax.fori_loop(0, 4, project_tile, 0)

    def activate(n, carry):
        t = lax.rem(n + 4, TILES)
        await_bytes(p_in.at[t], pr.at[t])
        both = p_own[t] + p_in[t]
        gate, up = both[:UNITS], both[UNITS:]
        hid[t, dp] = (gate / (1.0 + jnp.exp(-gate)) * up).astype(BF)
        for i in range(1, 8):
            remote(hid.at[t, dp], hid.at[t, dp], snd.at[5], hr.at[t], peer(i)).start()
        return carry

    lax.fori_loop(0, TILES, activate, 0)

    def produce(t):
        await_bytes(hid.at[t, pl.ds(0, 7)], hr.at[t])
        return dot(hid[t].reshape(8 * UNITS, TILE), wd[...], TN).astype(BF)

    ext[...] = produce(4)

    def finish(j):
        rows = pl.ds(j * 16, 16)
        y_send[rows, :, :FEAT] = produce(j).reshape(16, MAIN, FEAT)
        for g in range(2):
            more = tall(ext[pl.ds(pl.multiple_of(j * 64 + g * 32, 32), 32), :])
            y_send[pl.ds(j * 16 + g * 8, 8), :, FEAT:] = dot(q8, more).astype(BF).reshape(8, MAIN, 128)
        return y_send.at[rows]

    def give_back(i, carry):
        ref = finish(lax.rem(col + i, 4))
        remote(ref, y_in.at[col], snd.at[6], rcv.at[2], near(i)).start()
        return carry

    lax.fori_loop(1, 4, give_back, 0)
    mine = pltpu.make_async_copy(finish(col), y_in.at[col], loc.at[3])
    mine.start()
    await_bytes(y_in.at[pl.ds(0, 3)], rcv.at[2])
    mine.wait()

    def combine(block, n):
        slot, at = picked(block)
        terms = ring[block, TOK:, 128:256].astype(F32)
        more = broad(dot(shuffle4(), y_in[:, n, :, FEAT:].reshape(64, 128), TN).astype(BF))
        rows = jnp.concatenate([y_in[:, n, :, :FEAT].reshape(64, FEAT), more], axis=0)
        share = jnp.zeros((TOK, FEAT), F32)
        for part in range(2):
            mix = jnp.where(at, over_rows(by_slot(slot, terms[8 * part : 8 * part + 8])), 0.0)
            share = share + dot(mix.astype(BF), rows, TN)
        return share

    def hand(s, share, come, go, sem, sent, device, first=False):
        for h in range(2):
            rows = pl.ds(64 * h, 64)
            total = share[64 * h : 64 * h + 64]
            if not first:
                await_bytes(come.at[s - 1, rows], sem.at[2 * s - 2 + h])
                total = total + come[s - 1, rows, :].astype(F32)
            go[s, rows, :] = total.astype(BF)
            remote(go.at[s, rows], come.at[s, rows], sent, sem.at[2 * s + h], device).start()

    def hand_up(s, share, first=False):
        hand(s, share, up_in, up_out, su, snd.at[7], above, first)

    def hand_down(s, share, first=False):
        hand(s, share, dn_in, dn_out, sd, snd.at[8], below, first)

    hand_up(0, combine(far, 15), True)
    hand_down(0, combine(lax.rem(z + 9, NZ), 13), True)

    def home(s, carry):
        hand_up(s, combine(lax.rem(z + 8 - s, NZ), 16 - 2 * s))
        hand_down(s, combine(lax.rem(z + 9 + s, NZ), 13 - 2 * s))
        return carry

    lax.fori_loop(1, 7, home, 0)
    hand_up(7, combine(lax.rem(z + 1, NZ), 2))
    share = combine(z, 0)
    for h in range(2):
        rows = pl.ds(64 * h, 64)
        await_bytes(dn_in.at[6, rows], sd.at[12 + h])
        total = share[64 * h : 64 * h + 64] + dn_in[6, rows, :].astype(F32)
        await_bytes(up_in.at[7, rows], su.at[14 + h])
        out[rows, :] = (total + up_in[7, rows, :].astype(F32)).astype(BF)

    await_bytes(ring.at[pl.ds(0, 8)], snd.at[0])
    await_bytes(ring.at[pl.ds(0, 7)], snd.at[1])
    await_bytes(x_all.at[pl.ds(0, 15 * NZ)], snd.at[2])
    trade.wait_send()
    await_bytes(p_in, snd.at[4])
    await_bytes(hid.at[:, pl.ds(0, 7)], snd.at[5])
    await_bytes(y_in.at[pl.ds(0, 3)], snd.at[6])
    await_bytes(up_out, snd.at[7])
    await_bytes(dn_out, snd.at[8])
    for c in early:
        c.wait()


def exchange_kernel(pair, gu, down, old_gu, old_down, got_gu, got_down, snd, rcv):
    me = lax.axis_index("expert")
    spouse = {"expert": lax.rem(me + NE // 2, NE)}

    @pl.when(lax.rem(me, NE // 2) == pair)
    def _():
        barrier = pltpu.get_barrier_semaphore()
        pl.semaphore_signal(barrier, inc=1, device_id=spouse, device_id_type=MESH)
        pl.semaphore_wait(barrier, 1)
        parts = [(gu, got_gu, (0, 1)), (gu, got_gu, (0, 0, pl.ds(48, 48))), (down, got_down, (0, pl.ds(384, 384)))]
        copies = [
            pltpu.make_async_remote_copy(
                src.at[at], dst.at[at], snd.at[n], rcv.at[n], device_id=spouse, device_id_type=MESH
            )
            for n, (src, dst, at) in enumerate(parts)
        ]
        for c in copies:
            c.start()
        for c in copies:
            c.wait()


def exchange(pair, gu, down, old_gu, old_down):
    hbm = pl.BlockSpec(memory_space=pl.ANY)
    return tuple(
        pl.pallas_call(
            functools.partial(exchange_kernel, pair),
            out_shape=[jax.ShapeDtypeStruct(old_gu.shape, BF), jax.ShapeDtypeStruct(old_down.shape, BF)],
            in_specs=[hbm] * 4,
            out_specs=[hbm] * 2,
            input_output_aliases={2: 0, 3: 1},
            scratch_shapes=[pltpu.SemaphoreType.DMA((3,)), pltpu.SemaphoreType.DMA((3,))],
            compiler_params=pltpu.CompilerParams(collective_id=1 + pair, has_side_effects=True),
            name="exchange",
        )(gu, down, old_gu, old_down)
    )


def body(tokens, expert_ids, route_weight, placement, swap_flag, gate_up, down_weight):
    vmem = pl.BlockSpec(memory_space=pltpu.VMEM)
    hbm = pl.BlockSpec(memory_space=pl.ANY)
    moe_out, totals, *got = pl.pallas_call(
        kernel,
        out_shape=[
            jax.ShapeDtypeStruct((TOK, FEAT), BF),
            jax.ShapeDtypeStruct((8, 128), F32),
            jax.ShapeDtypeStruct(gate_up.shape, BF),
            jax.ShapeDtypeStruct(down_weight.shape, BF),
        ],
        in_specs=[vmem, vmem, vmem, vmem, hbm, hbm],
        out_specs=[vmem, vmem, hbm, hbm],
        scratch_shapes=[
            pltpu.VMEM((NZ, TOK + 16, FEAT), BF),
            pltpu.VMEM((4, NZ, MAIN, WIDE), BF),
            pltpu.VMEM((4 * NE, MAIN, WIDE), BF),
            pltpu.VMEM((4, UNITS, 4 * FEAT), BF),
            pltpu.VMEM((8 * UNITS, FEAT), BF),
            pltpu.VMEM((TILES, 2 * UNITS, TILE), F32),
            pltpu.VMEM((TILES, 2 * UNITS, TILE), F32),
            pltpu.VMEM((TILES, 2 * UNITS, TILE), F32),
            pltpu.VMEM((TILES, 8, UNITS, TILE), BF),
            pltpu.VMEM((NE * EXT, FEAT), BF),
            pltpu.VMEM((NE, MAIN, WIDE), BF),
            pltpu.VMEM((4, NZ, MAIN, WIDE), BF),
            pltpu.VMEM((8, TOK, FEAT), BF),
            pltpu.VMEM((8, TOK, FEAT), BF),
            pltpu.VMEM((7, TOK, FEAT), BF),
            pltpu.VMEM((7, TOK, FEAT), BF),
            pltpu.SemaphoreType.DMA((11,)),
            pltpu.SemaphoreType.DMA((5,)),
            pltpu.SemaphoreType.DMA((16,)),
            pltpu.SemaphoreType.DMA((14,)),
            pltpu.SemaphoreType.DMA((TILES,)),
            pltpu.SemaphoreType.DMA((TILES,)),
            pltpu.SemaphoreType.DMA((16,)),
            pltpu.SemaphoreType.DMA((14,)),
            pltpu.SemaphoreType.DMA((4,)),
        ],
        compiler_params=pltpu.CompilerParams(
            collective_id=0, has_side_effects=True, vmem_limit_bytes=48 << 20
        ),
        cost_estimate=pl.CostEstimate(flops=5_000_000_000, bytes_accessed=10_000_000, transcendentals=200_000),
        name="experts",
    )(tokens, expert_ids, route_weight, placement.reshape(1, NE), gate_up, down_weight)
    word = jnp.sum(swap_flag[: NE // 2] << jnp.arange(NE // 2, dtype=jnp.int32))
    word = lax.optimization_barrier(word)
    for pair in range(NE // 2):
        got = lax.cond(
            (word >> pair) & 1 == 1,
            functools.partial(exchange, pair),
            lambda gu, down, got_gu, got_down: (got_gu, got_down),
            gate_up, down_weight, *got,
        )
    got_gu, got_down = got
    flags = jnp.concatenate([swap_flag, swap_flag]) == 1
    load = totals[0, :NE]
    column_load = jnp.where(flags, jnp.roll(load, NE // 2), load) / jnp.float32(TOK * 8)
    mine = jnp.arange(NE // 2, dtype=jnp.int32) == lax.axis_index("expert") % (NE // 2)
    swapped = jnp.sum(jnp.where(mine, swap_flag, 0)) == 1
    return (
        moe_out,
        column_load,
        jnp.where(swapped, got_gu, gate_up),
        jnp.where(swapped, got_down, down_weight),
    )


def solution(mesh):
    return jax.shard_map(
        body,
        mesh=mesh,
        in_specs=(
            P("expert", "dp"),
            P("expert", None),
            P("expert", None),
            P(),
            P(),
            P("expert", None, "dp", None),
            P("expert", None, "dp"),
        ),
        out_specs=(P("expert", "dp"), P(), P("expert", None, "dp", None), P("expert", None, "dp")),
        check_vma=False,
    )
```

```python
import functools

import jax
import jax.numpy as jnp
from jax import lax
from jax.experimental import pallas as pl
from jax.experimental.pallas import tpu as pltpu
from jax.sharding import PartitionSpec as P

MESH = pl.DeviceIdType.MESH
BF = jnp.bfloat16
F32 = jnp.float32
NN = (((1,), (0,)), ((), ()))
NT = (((1,), (1,)), ((), ()))
TN = (((0,), (0,)), ((), ()))

NE = 64
NZ = 16
TOK = 128
FEAT = 512
MAIN, EXT = 16, 4
WIDE = FEAT + 128
UNITS = 96
TILE = 256
TILES = 5


def iota(shape, axis):
    return lax.broadcasted_iota(jnp.int32, shape, axis)


def flag(cond):
    return jnp.where(cond, 1.0, 0.0).astype(BF)


def dot(a, b, dims=NN):
    return lax.dot_general(a, b, dims, preferred_element_type=F32)


def shuffle8():
    row, col = iota((128, 128), 0), iota((128, 128), 1)
    return flag(((row % 16) // 4) * 32 + (row // 16) * 4 + row % 4 == col)


def shuffle4():
    row, col = iota((64, 64), 0), iota((64, 64), 1)
    return flag(((row % 16) // 4) * 16 + (row // 16) * 4 + row % 4 == col)


def tall(rows):
    return jnp.concatenate([rows[:, 128 * c : 128 * c + 128] for c in range(4)], axis=0)


def broad(rows):
    n = rows.shape[0] // 4
    return jnp.concatenate([rows[n * c : n * c + n] for c in range(4)], axis=1)


def over_rows(values):
    row = iota((16, TOK), 0) // EXT
    last = sum(jnp.where(row == j, values[j], 0.0) for j in range(4))
    return jnp.concatenate([jnp.broadcast_to(v, (MAIN, TOK)) for v in values] + [last], axis=0)


def row_number():
    row = iota((80, TOK), 0)
    return jnp.where(row < 64, row % MAIN, MAIN + row % EXT).astype(F32)


def kernel(
    tokens, ids, weight, place, gu, down,
    out, totals, got_gu, got_down,
    ring, pick, x_all, w, wd, p_send, p_own, p_in, hid, ext, y_send, y_in, up_out, up_in, dn_out, dn_in,
    snd, rcv, ru, rd, pr, hr, su, sd, loc,
):
    dp, me = lax.axis_index("dp"), lax.axis_index("expert")
    z, col = me // 4, lax.rem(me, 4)
    above, below = {"expert": lax.rem(me + 4, NE)}, {"expert": lax.rem(me + NE - 4, NE)}
    spouse = {"expert": lax.rem(me + 32, NE)}

    yh, xx = dp // 4, lax.rem(dp, 4)
    across = {"dp": lax.rem(dp + 4, 8)}

    def near(i, k=0):
        return {"dp": yh * 4 + lax.rem(xx + k, 4), "expert": z * 4 + lax.rem(col + i, 4)}

    def peer(i):
        return {"dp": lax.rem(dp + i, 8)}

    def remote(src, dst, send, recv, device):
        return pltpu.make_async_remote_copy(src, dst, send, recv, device_id=device, device_id_type=MESH)

    def await_bytes(ref, sem):
        pltpu.make_async_copy(ref, ref, sem).wait()

    barrier = pltpu.get_barrier_semaphore()
    others = [above, below, spouse] + [near(n % 4, n // 4) for n in range(1, 16)]
    others += [{"dp": (1 - yh) * 4 + lax.rem(xx + k, 4)} for k in range(4)]
    for device in others:
        pl.semaphore_signal(barrier, inc=1, device_id=device, device_id_type=MESH)

    half = pl.ds(pl.multiple_of(yh * 2048, 2048), 2048)
    other_half = pl.ds(pl.multiple_of((1 - yh) * 2048, 2048), 2048)
    local = [
        pltpu.make_async_copy(gu.at[0, :, :, half], w.at[pl.ds(0, 2)], loc.at[0]),
        pltpu.make_async_copy(down.at[0], wd, loc.at[1]),
    ]
    for c in local:
        c.start()

    lane = iota((TOK, 128), 1)
    place_f = place[...].astype(F32)
    hi = weight[...].astype(BF).astype(F32)
    lo = (weight[...] - hi).astype(BF).astype(F32)
    slots = []
    has = jnp.zeros((TOK, 128), F32)
    facts = jnp.zeros((TOK, 128), F32)
    for k in range(8):
        hit = ids[:, k : k + 1] == iota((TOK, NE), 1)
        slot = jnp.sum(jnp.where(hit, place_f, 0.0), axis=1, keepdims=True)
        slots.append(slot)
        has = has + jnp.where(slot == lane.astype(F32), 1.0, 0.0)
        facts = facts + jnp.where(lane == k, slot, 0.0)
        facts = facts + jnp.where(lane == 16 + k, hi[:, k : k + 1], 0.0) + jnp.where(lane == 24 + k, lo[:, k : k + 1], 0.0)
    before = flag(iota((TOK, TOK), 1) < iota((TOK, TOK), 0))
    count = dot(before, has.astype(BF))
    for k in range(8):
        pos = jnp.sum(jnp.where(slots[k] == lane.astype(F32), count, 0.0), axis=1, keepdims=True)
        facts = facts + jnp.where(lane == 8 + k, pos, 0.0)
    turned = dot(facts.astype(BF), flag(iota((TOK, TOK), 0) == iota((TOK, TOK), 1)), TN).astype(BF)
    ring[z, :TOK, :] = tokens[...]
    ring[z, TOK:, 0:128] = turned[0:16]
    ring[z, TOK:, 128:256] = turned[16:32]
    ring[z, TOK:, 256:384] = jnp.zeros((16, 128), BF)
    early = [
        remote(gu.at[0, 0, pl.ds(0, 48)], got_gu.at[0, 0, pl.ds(0, 48)], snd.at[9], rcv.at[3], spouse),
        remote(down.at[0, pl.ds(0, 384)], got_down.at[0, pl.ds(0, 384)], snd.at[10], rcv.at[4], spouse),
    ]
    ring[z, TOK:, 384:512] = dot(flag(iota((16, TOK), 0) == 0), has.astype(BF)).astype(BF)

    pl.semaphore_wait(barrier, len(others))

    def part_of(block, h):
        return ring.at[block, pl.ds(80 * h, 80 - 16 * h)]

    def pass_up(block, s, h):
        remote(part_of(block, h), part_of(block, h), snd.at[0], ru.at[2 * s + h], above).start()

    def pass_down(block, s, h):
        remote(part_of(block, h), part_of(block, h), snd.at[1], rd.at[2 * s + h], below).start()

    for h in range(2):
        pass_up(z, 0, h)
        pass_down(z, 0, h)
    trade = remote(gu.at[0, :, :, other_half], w.at[pl.ds(2, 2)], snd.at[3], rcv.at[1], across)
    trade.start()

    def by_slot(facts, values):
        return [
            jnp.sum(jnp.where(facts == (z * 4 + j).astype(F32), values, 0.0), axis=0, keepdims=True) for j in range(4)
        ]

    def picked(block):
        facts = ring[block, TOK:, 0:128].astype(F32)
        slot = facts[0:8]
        places = [v - 1.0 for v in by_slot(slot, facts[8:16] + 1.0)]
        return slot, over_rows(places) == row_number()

    def choose(block, n):
        rows = dot(flag(picked(block)[1]), ring[block, :TOK, :])
        more = rows[64:]
        third = flag((iota((16, 16), 0) % EXT == 3) & (iota((16, 16), 1) == 0))
        tally = dot(third, ring[block, TOK:, 384:512])
        more = tall(jnp.concatenate([more[:, :128] + tally, more[:, 128:]], axis=1)).astype(BF)
        pick[:, n, :, :FEAT] = rows[:64].astype(BF).reshape(4, MAIN, FEAT)
        pick[:, n, :, FEAT:] = dot(shuffle4(), more).astype(BF).reshape(4, MAIN, 128)

    def deal(n, blocks):
        src, dst = pl.ds(n, blocks), pl.ds(xx * NE + col * NZ + n, blocks)
        for m in range(1, 16):
            i, k = m % 4, m // 4
            j = lax.rem(col + i, 4)
            remote(pick.at[j, src], x_all.at[dst], snd.at[2], rcv.at[0], near(i, k)).start()
        pltpu.make_async_copy(pick.at[col, src], x_all.at[dst], loc.at[2]).start()

    choose(z, 0)
    deal(0, 1)

    def around(s, carry):
        low, high = lax.rem(z + 15 - s, NZ), lax.rem(z + 1 + s, NZ)
        for h in range(2):
            await_bytes(part_of(low, h), ru.at[2 * s + h])
            pass_up(low, s + 1, h)
            await_bytes(part_of(high, h), rd.at[2 * s + h])

            @pl.when(s < 6)
            def _(h=h):
                pass_down(high, s + 1, h)

        choose(low, 2 * s + 1)
        choose(high, 2 * s + 2)
        deal(2 * s + 1, 2)
        return carry

    lax.fori_loop(0, 7, around, 0)
    far = lax.rem(z + 8, NZ)
    for h in range(2):
        await_bytes(part_of(far, h), ru.at[14 + h])
    choose(far, 15)
    deal(15, 1)

    for c in local:
        c.wait()
    trade.wait_recv()
    await_bytes(x_all.at[pl.ds(0, 15 * NZ)], rcv.at[0])
    await_bytes(x_all.at[pl.ds(0, NZ)], loc.at[2])
    for c in early:
        c.start()

    q8 = shuffle8()

    def project(t, rows_of):
        total = jnp.zeros((4 * UNITS, TILE), F32)
        for x in range(4):
            part = w[:, :, x * FEAT : x * FEAT + FEAT].reshape(4 * UNITS, FEAT)
            total = total + dot(part, rows_of(x), NT)
        p_own[t] = total[: 2 * UNITS]
        p_send[t] = total[2 * UNITS :]
        remote(p_send.at[t], p_in.at[t], snd.at[4], pr.at[t], across).start()

    def further_rows(x):
        for b in range(8):
            packed = x_all[x * NE + 8 * b : x * NE + 8 * b + 8, :, FEAT:].reshape(128, 128)
            ext[32 * b : 32 * b + 32, :] = broad(dot(q8, packed, TN).astype(BF))
        if x == 0:
            totals[...] = dot(flag(iota((8, NE * EXT), 1) % EXT == 3), ext[:, :128])
        return ext[...]

    def project_tile(t, carry):
        project(t, lambda x: x_all[pl.ds(x * NE + t * 16, 16), :, :FEAT].reshape(TILE, FEAT))
        return carry

    project(4, further_rows)
    lax.fori_loop(0, 4, project_tile, 0)

    def activate(n, carry):
        t = lax.rem(n + 4, TILES)
        await_bytes(p_in.at[t], pr.at[t])
        both = p_own[t] + p_in[t]
        gate, up = both[:UNITS], both[UNITS:]
        hid[t, dp] = (gate / (1.0 + jnp.exp(-gate)) * up).astype(BF)
        for i in range(1, 8):
            remote(hid.at[t, dp], hid.at[t, dp], snd.at[5], hr.at[t], peer(i)).start()
        return carry

    lax.fori_loop(0, TILES, activate, 0)

    def produce(t):
        await_bytes(hid.at[t, pl.ds(0, 7)], hr.at[t])
        return dot(hid[t].reshape(8 * UNITS, TILE), wd[...], TN).astype(BF)

    ext[...] = produce(4)

    def finish(j):
        rows = pl.ds(j * 16, 16)
        y_send[rows, :, :FEAT] = produce(j).reshape(16, MAIN, FEAT)
        for g in range(2):
            more = tall(ext[pl.ds(pl.multiple_of(j * 64 + g * 32, 32), 32), :])
            y_send[pl.ds(j * 16 + g * 8, 8), :, FEAT:] = dot(q8, more).astype(BF).reshape(8, MAIN, 128)
        return y_send.at[rows]

    def give_back(i, carry):
        ref = finish(lax.rem(col + i, 4))
        remote(ref, y_in.at[col], snd.at[6], rcv.at[2], near(i)).start()
        return carry

    lax.fori_loop(1, 4, give_back, 0)
    mine = pltpu.make_async_copy(finish(col), y_in.at[col], loc.at[3])
    mine.start()
    await_bytes(y_in.at[pl.ds(0, 3)], rcv.at[2])
    mine.wait()

    def combine(block, n):
        slot, at = picked(block)
        terms = ring[block, TOK:, 128:256].astype(F32)
        more = broad(dot(shuffle4(), y_in[:, n, :, FEAT:].reshape(64, 128), TN).astype(BF))
        rows = jnp.concatenate([y_in[:, n, :, :FEAT].reshape(64, FEAT), more], axis=0)
        share = jnp.zeros((TOK, FEAT), F32)
        for part in range(2):
            mix = jnp.where(at, over_rows(by_slot(slot, terms[8 * part : 8 * part + 8])), 0.0)
            share = share + dot(mix.astype(BF), rows, TN)
        return share

    def hand(s, share, come, go, sem, sent, device, first=False):
        for h in range(2):
            rows = pl.ds(64 * h, 64)
            total = share[64 * h : 64 * h + 64]
            if not first:
                await_bytes(come.at[s - 1, rows], sem.at[2 * s - 2 + h])
                total = total + come[s - 1, rows, :].astype(F32)
            go[s, rows, :] = total.astype(BF)
            remote(go.at[s, rows], come.at[s, rows], sent, sem.at[2 * s + h], device).start()

    def hand_up(s, share, first=False):
        hand(s, share, up_in, up_out, su, snd.at[7], above, first)

    def hand_down(s, share, first=False):
        hand(s, share, dn_in, dn_out, sd, snd.at[8], below, first)

    hand_up(0, combine(far, 15), True)
    hand_down(0, combine(lax.rem(z + 9, NZ), 13), True)

    def home(s, carry):
        hand_up(s, combine(lax.rem(z + 8 - s, NZ), 16 - 2 * s))
        hand_down(s, combine(lax.rem(z + 9 + s, NZ), 13 - 2 * s))
        return carry

    lax.fori_loop(1, 7, home, 0)
    hand_up(7, combine(lax.rem(z + 1, NZ), 2))
    share = combine(z, 0)
    for h in range(2):
        rows = pl.ds(64 * h, 64)
        await_bytes(dn_in.at[6, rows], sd.at[12 + h])
        total = share[64 * h : 64 * h + 64] + dn_in[6, rows, :].astype(F32)
        await_bytes(up_in.at[7, rows], su.at[14 + h])
        out[rows, :] = (total + up_in[7, rows, :].astype(F32)).astype(BF)

    await_bytes(ring.at[pl.ds(0, 8)], snd.at[0])
    await_bytes(ring.at[pl.ds(0, 7)], snd.at[1])
    await_bytes(x_all.at[pl.ds(0, 15 * NZ)], snd.at[2])
    trade.wait_send()
    await_bytes(p_in, snd.at[4])
    await_bytes(hid.at[:, pl.ds(0, 7)], snd.at[5])
    await_bytes(y_in.at[pl.ds(0, 3)], snd.at[6])
    await_bytes(up_out, snd.at[7])
    await_bytes(dn_out, snd.at[8])
    for c in early:
        c.wait()


def exchange_kernel(pair, gu, down, old_gu, old_down, got_gu, got_down, snd, rcv):
    me = lax.axis_index("expert")
    spouse = {"expert": lax.rem(me + NE // 2, NE)}

    @pl.when(lax.rem(me, NE // 2) == pair)
    def _():
        barrier = pltpu.get_barrier_semaphore()
        pl.semaphore_signal(barrier, inc=1, device_id=spouse, device_id_type=MESH)
        pl.semaphore_wait(barrier, 1)
        parts = [(gu, got_gu, (0, 1)), (gu, got_gu, (0, 0, pl.ds(48, 48))), (down, got_down, (0, pl.ds(384, 384)))]
        copies = [
            pltpu.make_async_remote_copy(
                src.at[at], dst.at[at], snd.at[n], rcv.at[n], device_id=spouse, device_id_type=MESH
            )
            for n, (src, dst, at) in enumerate(parts)
        ]
        for c in copies:
            c.start()
        for c in copies:
            c.wait()


def exchange(pair, gu, down, old_gu, old_down):
    hbm = pl.BlockSpec(memory_space=pl.ANY)
    return tuple(
        pl.pallas_call(
            functools.partial(exchange_kernel, pair),
            out_shape=[jax.ShapeDtypeStruct(old_gu.shape, BF), jax.ShapeDtypeStruct(old_down.shape, BF)],
            in_specs=[hbm] * 4,
            out_specs=[hbm] * 2,
            input_output_aliases={2: 0, 3: 1},
            scratch_shapes=[pltpu.SemaphoreType.DMA((3,)), pltpu.SemaphoreType.DMA((3,))],
            compiler_params=pltpu.CompilerParams(collective_id=1 + pair, has_side_effects=True),
            name="exchange",
        )(gu, down, old_gu, old_down)
    )


def body(tokens, expert_ids, route_weight, placement, swap_flag, gate_up, down_weight):
    vmem = pl.BlockSpec(memory_space=pltpu.VMEM)
    hbm = pl.BlockSpec(memory_space=pl.ANY)
    moe_out, totals, *got = pl.pallas_call(
        kernel,
        out_shape=[
            jax.ShapeDtypeStruct((TOK, FEAT), BF),
            jax.ShapeDtypeStruct((8, 128), F32),
            jax.ShapeDtypeStruct(gate_up.shape, BF),
            jax.ShapeDtypeStruct(down_weight.shape, BF),
        ],
        in_specs=[vmem, vmem, vmem, vmem, hbm, hbm],
        out_specs=[vmem, vmem, hbm, hbm],
        scratch_shapes=[
            pltpu.VMEM((NZ, TOK + 16, FEAT), BF),
            pltpu.VMEM((4, NZ, MAIN, WIDE), BF),
            pltpu.VMEM((4 * NE, MAIN, WIDE), BF),
            pltpu.VMEM((4, UNITS, 4 * FEAT), BF),
            pltpu.VMEM((8 * UNITS, FEAT), BF),
            pltpu.VMEM((TILES, 2 * UNITS, TILE), F32),
            pltpu.VMEM((TILES, 2 * UNITS, TILE), F32),
            pltpu.VMEM((TILES, 2 * UNITS, TILE), F32),
            pltpu.VMEM((TILES, 8, UNITS, TILE), BF),
            pltpu.VMEM((NE * EXT, FEAT), BF),
            pltpu.VMEM((NE, MAIN, WIDE), BF),
            pltpu.VMEM((4, NZ, MAIN, WIDE), BF),
            pltpu.VMEM((8, TOK, FEAT), BF),
            pltpu.VMEM((8, TOK, FEAT), BF),
            pltpu.VMEM((7, TOK, FEAT), BF),
            pltpu.VMEM((7, TOK, FEAT), BF),
            pltpu.SemaphoreType.DMA((11,)),
            pltpu.SemaphoreType.DMA((5,)),
            pltpu.SemaphoreType.DMA((16,)),
            pltpu.SemaphoreType.DMA((14,)),
            pltpu.SemaphoreType.DMA((TILES,)),
            pltpu.SemaphoreType.DMA((TILES,)),
            pltpu.SemaphoreType.DMA((16,)),
            pltpu.SemaphoreType.DMA((14,)),
            pltpu.SemaphoreType.DMA((4,)),
        ],
        compiler_params=pltpu.CompilerParams(
            collective_id=0, has_side_effects=True, vmem_limit_bytes=48 << 20
        ),
        cost_estimate=pl.CostEstimate(flops=5_000_000_000, bytes_accessed=10_000_000, transcendentals=200_000),
        name="experts",
    )(tokens, expert_ids, route_weight, placement.reshape(1, NE), gate_up, down_weight)
    word = jnp.sum(swap_flag[: NE // 2] << jnp.arange(NE // 2, dtype=jnp.int32))
    word = lax.optimization_barrier(word)
    for pair in range(NE // 2):
        got = lax.cond(
            (word >> pair) & 1 == 1,
            functools.partial(exchange, pair),
            lambda gu, down, got_gu, got_down: (got_gu, got_down),
            gate_up, down_weight, *got,
        )
    got_gu, got_down = got
    flags = jnp.concatenate([swap_flag, swap_flag]) == 1
    load = totals[0, :NE]
    column_load = jnp.where(flags, jnp.roll(load, NE // 2), load) / jnp.float32(TOK * 8)
    mine = jnp.arange(NE // 2, dtype=jnp.int32) == lax.axis_index("expert") % (NE // 2)
    swapped = jnp.sum(jnp.where(mine, swap_flag, 0)) == 1
    return (
        moe_out,
        column_load,
        jnp.where(swapped, got_gu, gate_up),
        jnp.where(swapped, got_down, down_weight),
    )


def solution(mesh):
    return jax.shard_map(
        body,
        mesh=mesh,
        in_specs=(
            P("expert", "dp"),
            P("expert", None),
            P("expert", None),
            P(),
            P(),
            P("expert", None, "dp", None),
            P("expert", None, "dp"),
        ),
        out_specs=(P("expert", "dp"), P(), P("expert", None, "dp", None), P("expert", None, "dp")),
        check_vma=False,
    )
```
